256 devices in a mesh: section: 8 (over x, z_hi), dp: 32 (over z_lo, y, core).
Axes of the slice: x: 4, y: 4, z: 8 (z_hi: 2, z_lo: 4; z = z_hi * 4 + z_lo), core: 2. Of those that a mesh axis runs over, the one named last changes fastest.
Arguments:
- text: bfloat16 [6144, 8192], P('dp'), may hold values from -60 to 60
- image: bfloat16 [1536, 3200], P('dp'), may hold values from -60 to 60
- positions: int32 [96, 16], P('dp'), may hold values from 0 to 63, as said below
- enc_in: bfloat16 [8, 3200, 128], P('section', 'dp'), may hold values from -0.109375 to 0.109375
- enc_out: bfloat16 [8, 128, 3200], P('section', None, 'dp'), may hold values from -0.5 to 0.5
- conn_in: bfloat16 [3200, 64], P('dp'), may hold values from -0.109375 to 0.109375
- conn_out: bfloat16 [64, 8192], P(None, 'dp'), may hold values from -0.75 to 0.75
- llm_in: bfloat16 [8, 8192, 512], P('section', 'dp'), may hold values from -0.0625 to 0.0625
- llm_out: bfloat16 [8, 512, 8192], P('section', None, 'dp'), may hold values from -0.25 to 0.25
Outputs:
- layer_states: bfloat16 [8, 6144, 8192], P('section', 'dp')
The draws below stay inside these ranges and needn't reach their ends.
Inputs may be any that keep to these rules, and one draw needn't show every extreme that they name: Each row holds 16 distinct positions within one micro-batch of 64 rows, in ascending order.
All inputs are finite; a program needn't handle non-finite values.
Results may differ from the reference program's by a relative error of at most 0.009.
Values may be sent and summed in bfloat16 or wider, within the bound.
A program may use at most 128 MiB of HBM per device.

```python
import math
import jax
import jax.numpy as jnp
from jax import lax

D = 8192
DV = 3200
RANK = 512
ENC_RANK = 128
CONN_RANK = 64
ROWS = 64
IMG = 16
LAYER_COUNT = 8
MB_ALL = 96
TEXT_ROWS = 6144
IMG_ROWS = 1536


def scaled_field(key, row_count, col_count):
    first, second, third = jax.random.split(key, 3)
    base = jnp.clip(jax.random.normal(first, (row_count, col_count), jnp.float32), -4.0, 4.0)
    per_row_scale = jnp.exp(jax.random.uniform(second, (row_count, 1), jnp.float32, math.log(0.3), math.log(3.0)))
    col_scale = jnp.exp(jax.random.uniform(third, (1, col_count), jnp.float32, math.log(0.5), math.log(5.0)))
    return (base * per_row_scale * col_scale).astype(jnp.bfloat16)


def draw_text(key, part):
    return scaled_field(jax.random.fold_in(key, 11), TEXT_ROWS, D)


def draw_image(key, part):
    return scaled_field(jax.random.fold_in(key, 23), IMG_ROWS, DV)


def draw_positions(key, part):
    row_keys = jax.random.split(jax.random.fold_in(key, 37), MB_ALL)

    def one_row(random_row_key):
        shuffled = jax.random.permutation(random_row_key, ROWS)
        return jnp.sort(shuffled[:IMG]).astype(jnp.int32)
    return jax.vmap(one_row)(row_keys)


def shard_levels(stream_key, extent, cuts, low, top_value):
    level, own = 1.0, jax.random.fold_in(stream_key, 6)
    for position, blocks in cuts:
        heights = jnp.exp(jax.random.uniform(jax.random.fold_in(own, position), (blocks,), jnp.float32, low / len(cuts), top_value / len(cuts)))
        level = level * jnp.repeat(heights, extent[position] // blocks).reshape([-1 if axis == position else 1 for axis in range(len(extent))])
    return level


def normal_values(rng, extent, spread, limit, cuts=(), kind=jnp.bfloat16):
    result = spread * jax.random.normal(rng, extent, jnp.float32)
    if cuts:
        result = result * shard_levels(rng, extent, cuts, -0.22, 0.18)
    return jnp.clip(result, -limit, limit).astype(kind)


def setup_inputs(seed: int = 0) -> dict:
    splits = jax.random.split(jax.random.key(seed), 10)
    return {
        "text": draw_text(jax.random.fold_in(splits[9], 71), 0),
        "image": draw_image(jax.random.fold_in(splits[9], 71), 0),
        "positions": draw_positions(jax.random.fold_in(splits[9], 71), 0),
        "enc_in": normal_values(splits[3], (LAYER_COUNT, DV, ENC_RANK), DV ** -0.5, 0.109375, ((0, 8), (1, 32))),
        "enc_out": normal_values(splits[4], (LAYER_COUNT, ENC_RANK, DV), ENC_RANK ** -0.5, 0.5, ((0, 8), (2, 32))),
        "conn_in": normal_values(splits[5], (DV, CONN_RANK), DV ** -0.5, 0.109375, ((0, 32),)),
        "conn_out": normal_values(splits[6], (CONN_RANK, D), CONN_RANK ** -0.5, 0.75, ((1, 32),)),
        "llm_in": normal_values(splits[7], (LAYER_COUNT, D, RANK), D ** -0.5, 0.0625, ((0, 8), (1, 32))),
        "llm_out": normal_values(splits[8], (LAYER_COUNT, RANK, D), RANK ** -0.5, 0.25, ((0, 8), (2, 32))),
    }


EPSILON = 1e-06

def normed_rows(expanded_rows):
    scale = lax.rsqrt(lax.optimization_barrier(jnp.mean(expanded_rows * expanded_rows, axis=-1, keepdims=True)) + EPSILON)
    return (expanded_rows * scale).astype(jnp.bfloat16)

def encoder_act(values):
    return jax.nn.gelu(values, approximate=False)

def adapter_layer(hidden, weight_in, weight_out, nonlinear):
    expanded_rows = hidden.astype(jnp.float32)
    normed = normed_rows(expanded_rows)
    projected = jnp.dot(normed, weight_in, preferred_element_type=jnp.float32)
    activated = nonlinear(projected).astype(jnp.bfloat16)
    branch = jnp.dot(activated, weight_out, preferred_element_type=jnp.float32)
    return (expanded_rows + branch).astype(jnp.bfloat16)

def reference(text, image, positions, enc_in, enc_out, conn_in, conn_out, llm_in, llm_out):
    encoded = image
    for layer_index in range(LAYER_COUNT):
        encoded = adapter_layer(encoded, enc_in[layer_index], enc_out[layer_index], encoder_act)
    latent = encoder_act(jnp.dot(normed_rows(encoded.astype(jnp.float32)), conn_in, preferred_element_type=jnp.float32)).astype(jnp.bfloat16)
    picture_row_block = jnp.dot(latent, conn_out, preferred_element_type=jnp.float32).astype(jnp.bfloat16)
    picture_row_block = picture_row_block.reshape(MB_ALL, IMG, D)
    state = text.reshape(MB_ALL, ROWS, D)
    batch_index = jnp.broadcast_to(jnp.arange(MB_ALL, dtype=jnp.int32)[:, None], (MB_ALL, IMG))
    state = state.at[batch_index, positions.astype(jnp.int32)].set(picture_row_block)
    state = state.reshape(MB_ALL * ROWS, D)
    hidden_state_list = []
    for layer_index in range(LAYER_COUNT):
        state = adapter_layer(state, llm_in[layer_index], llm_out[layer_index], jax.nn.silu)
        hidden_state_list.append(state)
    return jnp.stack(hidden_state_list)
```

```python
import jax
import jax.numpy as jnp
from jax import lax
from jax.experimental import pallas as pl
from jax.experimental.pallas import tpu as pltpu
from jax.sharding import PartitionSpec as P

EPSILON = 1e-06
MESH = pl.DeviceIdType.MESH
F32 = jnp.float32
BF16 = jnp.bfloat16
CHUNKS = 6
BLOCKS = 16


def gelu(v):
    return 0.5 * v * (1.0 + lax.erf(v * 0.7071067811865476))


def silu(v):
    return v / (1.0 + jnp.exp(-v))


def matmul(a, b):
    return jnp.dot(a, b, preferred_element_type=F32)


def device(x, y, z, c):
    return (x * 2 + z // 4, lax.rem(z, 4) * 8 + y * 2 + c)


def kernel(
    text, wa, wb, e3, img, oh, out,
    A, B, E1, E2, h0, ohb, henc, lat, latr, imgrows, xs, xr, es, er, hin, osend, orecv,
    send, recv_llm, recv_enc, own_sem, gather_s, gather_r, text_l, text_s, text_r,
    misc_s, misc_r, x_s, x_r, xe_s, xe_r, flow_s, flow_r, out_s, out_r,
):
    section = lax.axis_index("section")
    dp = lax.axis_index("dp")
    x, z_hi = section // 2, lax.rem(section, 2)
    z = z_hi * 4 + dp // 8
    y = lax.rem(dp // 2, 4)
    c = lax.rem(dp, 2)
    o = 1 - c
    me = z * 4 + y

    def up(v, by, n):
        return lax.rem(v + by + n, n)

    y_up, y_down = device(x, up(y, 1, 4), z, c), device(x, up(y, -1, 4), z, c)
    z_up, z_down = device(x, y, up(z, 1, 8), c), device(x, y, up(z, -1, 8), c)
    other = device(x, y, z, o)
    x_next = device(up(x, 1, 4), y, z, c)
    plane3, plane0 = device(3, y, z, c), device(0, y, z, c)

    def remote(src, dst, ssem, rsem, to):
        return pltpu.make_async_remote_copy(
            src_ref=src, dst_ref=dst, send_sem=ssem, recv_sem=rsem, device_id=to, device_id_type=MESH
        )

    own = [
        pltpu.make_async_copy(wa, A.at[me], own_sem.at[0]),
        pltpu.make_async_copy(wb, B.at[me], own_sem.at[1]),
    ]
    for copy in own:
        copy.start()

    barrier = pltpu.get_barrier_semaphore()
    for to in (
        y_up, y_down, z_up, z_down, other, x_next,
        device(up(x, 2, 4), y, z, c), device(up(x, 3, 4), y, z, c),
    ):
        pl.semaphore_signal(barrier, inc=1, device_id=to, device_id_type=MESH)
    pl.semaphore_wait(barrier, 8)

    def to_plane3(k, place):
        return remote(e3.at[k], place.at[me, x], gather_s.at[k], gather_r.at[k, x], plane3)

    @pl.when(x != 3)
    def _():
        to_plane3(0, E1).start()
        to_plane3(1, E2).start()

    for copy in own:
        copy.wait()

    def relay(bufs, recv):
        sent = [0, 0]
        pending = []
        y_at = (y, up(y, -1, 4), up(y, 1, 4), up(y, 2, 4))

        def go(t, dz, i, *tos):
            slot = up(z, dz, 8) * 4 + y_at[i]
            for to in tos:
                copy = remote(
                    bufs[t].at[slot], bufs[t].at[slot], send.at[t, sent[t]], recv.at[t, slot], to
                )
                copy.start()
                pending.append(copy)
                sent[t] += 1

        def came(t, dz, i):
            slot = up(z, dz, 8) * 4 + y_at[i]
            remote(
                bufs[t].at[slot], bufs[t].at[slot], send.at[t, 0], recv.at[t, slot], y_up
            ).wait_recv()

        def across(place):
            dz = (0, -1, 1, -2, 2, -3, 3, 4)[place]
            came(1, dz, 1)
            if place % 2 == 0:
                go(1, dz, 1, y_up)
            came(1, dz, 2)
            if place % 2 == 1:
                go(1, dz, 2, y_down)

        go(0, 0, 0, z_up, z_down, y_up, y_down)
        go(1, 0, 0, y_up, y_down, z_up, z_down)
        came(0, 0, 1)
        go(0, 0, 1, y_up, z_up, z_down)
        came(0, 0, 2)
        go(0, 0, 2, z_up, z_down)
        for r in (1, 2, 3):
            came(1, -r, 0)
            go(1, -r, 0, *((z_up,) if r < 3 else ()), y_up, y_down)
            came(1, r, 0)
            go(1, r, 0, z_down, y_up, y_down)
            if r == 1:
                across(0)
                came(0, 0, 3)
                go(0, 0, 3, z_up, z_down)
            for i in range(4):
                came(0, -r, i)
                if r < 3 or i % 2 == 0:
                    go(0, -r, i, z_up)
                came(0, r, i)
                if r < 3 or i % 2 == 1:
                    go(0, r, i, z_down)
                if r > 1 and i == 1:
                    across(2 * r - 3)
            if r > 1:
                across(2 * r - 2)
        came(1, 4, 0)
        go(1, 4, 0, y_up, y_down)
        for place in (5, 6, 7):
            across(place)
        for i in range(4):
            came(0, 4, i)
        for dz in (0, -1, 1, -2, 2, -3, 3, 4):
            came(1, dz, 3)
        for copy in pending:
            copy.wait_send()

    def exchange(mine, theirs, ssem, rsem, slot):
        copy = remote(mine.at[slot], theirs.at[slot], ssem.at[slot], rsem.at[slot], other)
        copy.start()
        copy.wait()
        return mine[slot] + theirs[slot]

    @pl.when(x == 3)
    def _():
        mine = [
            pltpu.make_async_copy(e3.at[0], E1.at[me, 3], own_sem.at[2]),
            pltpu.make_async_copy(e3.at[1], E2.at[me, 3], own_sem.at[3]),
            pltpu.make_async_copy(e3.at[2], E1.at[me, 4], own_sem.at[4]),
            pltpu.make_async_copy(
                img.at[c], henc.at[pl.ds(pl.multiple_of(c * 48, 16), 48)], own_sem.at[5]
            ),
        ]
        for copy in mine:
            copy.start()
        rows = remote(
            img.at[o], henc.at[pl.ds(pl.multiple_of(c * 48, 16), 48)], misc_s.at[0], misc_r.at[0], other
        )
        rows.start()
        for copy in mine:
            copy.wait()
        for from_x in range(3):
            for k, place in ((0, E1), (1, E2)):
                remote(
                    e3.at[k], place.at[me, from_x], gather_s.at[k], gather_r.at[k, from_x], x_next
                ).wait_recv()
        relay((E1, E2), recv_enc)
        rows.wait()

        def projected(slot, first, k):
            h = henc[...]
            weight = E1[pl.ds(first, BLOCKS), k].reshape(BLOCKS * 128, 128)
            es[slot, :, 0:128] = matmul(h, weight)
            squares = jnp.zeros((96, 128), F32)
            for j in range(BLOCKS):
                part = h[:, j * 128 : (j + 1) * 128].astype(F32)
                squares += part * part
            es[slot, :, 128:256] = squares
            total = exchange(es, er, xe_s, xe_r, slot)
            scale = lax.rsqrt(
                jnp.sum(total[:, 128:256], axis=-1, keepdims=True) * (1.0 / 3200) + EPSILON
            )
            return gelu(total[:, 0:128] * scale).astype(BF16)

        def layer(l, _):
            first, k = lax.rem(l, 2) * BLOCKS, l // 2
            activated = projected(lax.rem(l, 2), first, k)
            for j in range(0, BLOCKS, 2):
                weight = E2[pl.ds(first + j, 2), k].reshape(256, 128)
                branch = lax.dot_general(
                    activated, weight, (((1,), (1,)), ((), ())), preferred_element_type=F32
                )
                cols = slice(j * 128, (j + 2) * 128)
                henc[:, cols] = (henc[:, cols].astype(F32) + branch).astype(BF16)
            return 0

        lax.fori_loop(0, 8, layer, 0)
        lat[...] = projected(0, 0, 4)
        copy = remote(lat, latr, misc_s.at[1], misc_r.at[1], plane0)
        copy.start()
        copy.wait_send()

    def text_local(j):
        return pltpu.make_async_copy(
            text.at[:, pl.ds(pl.multiple_of(j * 512 + c * 256, 256), 256)],
            h0.at[c, :, pl.ds(j * 256, 256)],
            text_l.at[j],
        )

    def text_other(j):
        return remote(
            text.at[:, pl.ds(pl.multiple_of(j * 512 + o * 256, 256), 256)],
            h0.at[c, :, pl.ds(j * 256, 256)],
            text_s.at[j], text_r.at[j], other,
        )

    def text_came(j):
        return remote(
            text.at[:, pl.ds(0, 256)],
            h0.at[o, :, pl.ds(j * 256, 256)],
            text_s.at[j], text_r.at[j], other,
        )

    oh_local = pltpu.make_async_copy(oh, ohb.at[c], own_sem.at[2])
    oh_other = remote(oh, ohb.at[c], misc_s.at[0], misc_r.at[0], other)

    @pl.when(x == 0)
    def _():
        oh_local.start()
        oh_other.start()
        for j in range(BLOCKS):
            text_local(j).start()
            text_other(j).start()

    relay((A, B), recv_llm)

    @pl.when(x == 0)
    def _():
        oh_local.wait()
        oh_other.wait_send()
        remote(oh, ohb.at[o], misc_s.at[0], misc_r.at[0], other).wait_recv()
        for j in range(BLOCKS):
            text_local(j).wait()
            text_other(j).wait_send()
            text_came(j).wait_recv()
        remote(lat, latr, misc_s.at[1], misc_r.at[1], x_next).wait_recv()
        imgrows[96:128, :] = jnp.zeros((32, BLOCKS * 256), BF16)
        latent = latr[:, 0:64]
        for j in range(BLOCKS):
            imgrows[0:96, j * 256 : (j + 1) * 256] = matmul(latent, B[j, 512:576, :]).astype(BF16)

    def cols(j):
        return pl.ds(pl.multiple_of(j * 256, 256), 256)

    def folded(v):
        return v[:, 0:128] * v[:, 0:128] + v[:, 128:256] * v[:, 128:256]

    def activation(slot, acc, squares):
        xs[slot, :, 0:512] = acc
        xs[slot, :, 512:640] = squares
        total = exchange(xs, xr, x_s, x_r, slot)
        scale = lax.rsqrt(
            jnp.sum(total[:, 512:640], axis=-1, keepdims=True) * (1.0 / 8192) + EPSILON
        )
        return silu(total[:, 0:512] * scale).astype(BF16)

    zeros = (jnp.zeros((64, 512), F32), jnp.zeros((64, 128), F32))

    def flow(k):
        return remote(hin.at[k], hin.at[k], flow_s.at[k], flow_r.at[k], x_next)

    def result(k):
        return remote(osend.at[k], orecv.at[k], out_s.at[k], out_r.at[k], other)

    def emit(k):
        rows = pl.ds(pl.multiple_of(k * 32, 32), 32)
        for j in range(BLOCKS):
            span = slice(j * 256, (j + 1) * 256)
            out[rows, pl.ds(pl.multiple_of(j * 512 + c * 256, 256), 256)] = hin[
                k, pl.ds(pl.multiple_of(c * 32, 32), 32), span
            ]
        osend[k] = hin[k, pl.ds(pl.multiple_of(o * 32, 32), 32), :]
        result(k).start()

    def merge(k):
        result(k).wait_recv()
        rows = pl.ds(pl.multiple_of(k * 32, 32), 32)
        for j in range(BLOCKS):
            out[rows, pl.ds(pl.multiple_of(j * 512 + o * 256, 256), 256)] = orecv[
                k, :, j * 256 : (j + 1) * 256
            ]

    def chunk(k, _):
        rows = pl.ds(pl.multiple_of(k * 32, 32), 32)

        @pl.when(x == 0)
        def _():
            marks = jnp.concatenate([ohb[0, rows, :], ohb[1, rows, :]], axis=0)
            hit = jnp.sum(marks.astype(F32), axis=-1, keepdims=True) > 0.5
            for j in range(BLOCKS):
                span = slice(j * 256, (j + 1) * 256)
                placed = matmul(marks, imgrows[:, span])
                words = jnp.concatenate([h0[0, rows, span], h0[1, rows, span]], axis=0)
                hin[k, :, span] = jnp.where(hit, placed, words.astype(F32)).astype(BF16)

        @pl.when(x > 0)
        def _():
            flow(k).wait_recv()

        def first(j, carry):
            acc, squares = carry
            h = hin[k, :, cols(j)]
            return acc + matmul(h, A[j]), squares + folded(h.astype(F32))

        a = activation(0, *lax.fori_loop(0, BLOCKS, first, zeros, unroll=4))

        def second(j, carry):
            acc, squares = carry
            h = hin[k, :, cols(j)].astype(F32) + matmul(a, B[j, 0:512, :])
            h = h.astype(BF16)
            hin[k, :, cols(j)] = h
            return acc + matmul(h, A[BLOCKS + j]), squares + folded(h.astype(F32))

        carry = lax.fori_loop(0, BLOCKS, second, zeros, unroll=4)

        @pl.when(z_hi == 0)
        def _():
            emit(k)

        b = activation(1, *carry)

        def third(j, _):
            h = hin[k, :, cols(j)].astype(F32) + matmul(b, B[BLOCKS + j, 0:512, :])
            hin[k, :, cols(j)] = h.astype(BF16)
            return 0

        lax.fori_loop(0, BLOCKS, third, 0, unroll=4)

        @pl.when(x < 3)
        def _():
            flow(k).start()

        @pl.when(z_hi == 1)
        def _():
            emit(k)

        @pl.when(k > 0)
        def _():
            merge(k - 1)

        return 0

    lax.fori_loop(0, CHUNKS, chunk, 0)
    merge(CHUNKS - 1)

    def drain(k, _):
        result(k).wait_send()

        @pl.when(x < 3)
        def _():
            flow(k).wait_send()

        return 0

    lax.fori_loop(0, CHUNKS, drain, 0)

    @pl.when(x != 3)
    def _():
        to_plane3(0, E1).wait_send()
        to_plane3(1, E2).wait_send()


def local(text, image, positions, enc_in, enc_out, conn_in, conn_out, llm_in, llm_out):
    core = lax.rem(lax.axis_index("dp"), 2)
    wb = jnp.concatenate([llm_out[0], conn_out], axis=0)
    e3 = jnp.stack(
        [
            jnp.pad(enc_in[0], ((0, 28), (0, 0))),
            jnp.pad(enc_out[0].T, ((0, 28), (0, 0))),
            jnp.pad(conn_in, ((0, 28), (0, 64))),
        ]
    )
    img = jnp.pad(image.reshape(48, 16, 2, 100), ((0, 0), (0, 0), (0, 0), (0, 28)))
    img = img.transpose(2, 0, 1, 3).reshape(2, 48, 2048)
    row = lax.broadcasted_iota(jnp.int32, (192, 48), 0)
    spots = (positions + 64 * jnp.arange(3, dtype=jnp.int32)[:, None]).reshape(1, 48)
    marks = (spots == row).astype(BF16)
    blank = jnp.zeros((192, 48), BF16)
    oh = jnp.concatenate(
        [
            jnp.where(core == 0, marks, blank),
            jnp.where(core == 1, marks, blank),
            jnp.zeros((192, 32), BF16),
        ],
        axis=1,
    )
    any_spec = pl.BlockSpec(memory_space=pl.ANY)
    dma = pltpu.SemaphoreType.DMA
    hidden = pl.pallas_call(
        kernel,
        out_shape=jax.ShapeDtypeStruct((192, 8192), BF16),
        in_specs=[any_spec] * 6,
        out_specs=pl.BlockSpec(memory_space=pltpu.VMEM),
        scratch_shapes=[
            pltpu.VMEM((32, 256, 512), BF16),
            pltpu.VMEM((32, 576, 256), BF16),
            pltpu.VMEM((32, 5, 128, 128), BF16),
            pltpu.VMEM((32, 4, 128, 128), BF16),
            pltpu.VMEM((2, 192, 4096), BF16),
            pltpu.VMEM((2, 192, 128), BF16),
            pltpu.VMEM((96, 2048), BF16),
            pltpu.VMEM((96, 128), BF16),
            pltpu.VMEM((96, 128), BF16),
            pltpu.VMEM((128, 4096), BF16),
            pltpu.VMEM((2, 64, 640), F32),
            pltpu.VMEM((2, 64, 640), F32),
            pltpu.VMEM((2, 96, 256), F32),
            pltpu.VMEM((2, 96, 256), F32),
            pltpu.VMEM((CHUNKS, 64, 4096), BF16),
            pltpu.VMEM((CHUNKS, 32, 4096), BF16),
            pltpu.VMEM((CHUNKS, 32, 4096), BF16),
            dma((2, 31)),
            dma((2, 32)),
            dma((2, 32)),
            dma((6,)),
            dma((2,)),
            dma((2, 4)),
            dma((16,)),
            dma((16,)),
            dma((16,)),
            dma((2,)),
            dma((2,)),
            dma((2,)),
            dma((2,)),
            dma((2,)),
            dma((2,)),
            dma((CHUNKS,)),
            dma((CHUNKS,)),
            dma((CHUNKS,)),
            dma((CHUNKS,)),
        ],
        compiler_params=pltpu.CompilerParams(
            collective_id=0, has_side_effects=True, vmem_limit_bytes=60 * 1024 * 1024
        ),
        cost_estimate=pl.CostEstimate(
            flops=14_000_000_000, bytes_accessed=16_000_000, transcendentals=1_000_000
        ),
    )(text, llm_in[0], wb, e3, img, oh)
    return hidden[None]


def solution(mesh):
    return jax.shard_map(
        local,
        mesh=mesh,
        in_specs=(
            P("dp", None),
            P("dp", None),
            P("dp", None),
            P("section", "dp", None),
            P("section", None, "dp"),
            P("dp", None),
            P(None, "dp"),
            P("section", "dp", None),
            P("section", None, "dp"),
        ),
        out_specs=P("section", "dp", None),
        check_vma=False,
    )
```

```python
import jax
import jax.numpy as jnp
from jax import lax
from jax.experimental import pallas as pl
from jax.experimental.pallas import tpu as pltpu
from jax.sharding import PartitionSpec as P

EPSILON = 1e-06
MESH = pl.DeviceIdType.MESH
F32 = jnp.float32
BF16 = jnp.bfloat16
SPLIT = 208
TURNS = ((1, 0.15), (2, 0.35), (3, 0.55))
BLOCKS = 16


def gelu(v):
    return 0.5 * v * (1.0 + lax.erf(v * 0.7071067811865476))


def silu(v):
    return v / (1.0 + jnp.exp(-v))


def matmul(a, b):
    return jnp.dot(a, b, preferred_element_type=F32)


def device(x, y, z, c):
    return (x * 2 + z // 4, lax.rem(z, 4) * 8 + y * 2 + c)


def kernel(
    text, image, positions, enc_in, enc_out, conn_in, conn_out, wa, wb, out,
    A, B, E1, E2, C1, C2, h0, ohb, img2, henc, imgrows, xs, xr, es, er, hin, osend, orecv,
    send_llm, recv_llm, send_enc, recv_enc, recv_conn, own_sem, text_l, text_s, text_r,
    misc_s, misc_r, x_s, x_r, xe_s, xe_r, flow_s, flow_r, out_s, out_r,
):
    section = lax.axis_index("section")
    dp = lax.axis_index("dp")
    x, z_hi = section // 2, lax.rem(section, 2)
    z = z_hi * 4 + dp // 8
    y = lax.rem(dp // 2, 4)
    c = lax.rem(dp, 2)
    o = 1 - c
    me = z * 4 + y

    def up(v, by, n):
        return lax.rem(v + by + n, n)

    y_up, y_down = device(x, up(y, 1, 4), z, c), device(x, up(y, -1, 4), z, c)
    z_up, z_down = device(x, y, up(z, 1, 8), c), device(x, y, up(z, -1, 8), c)
    other = device(x, y, z, o)
    x_next = device(up(x, 1, 4), y, z, c)
    x_last = device(up(x, -1, 4), y, z, c)

    def remote(src, dst, ssem, rsem, to):
        return pltpu.make_async_remote_copy(
            src_ref=src, dst_ref=dst, send_sem=ssem, recv_sem=rsem, device_id=to, device_id_type=MESH
        )

    barrier = pltpu.get_barrier_semaphore()
    for to in (y_up, y_down, z_up, z_down, other, x_next, x_last):
        pl.semaphore_signal(barrier, inc=1, device_id=to, device_id_type=MESH)

    own = [
        pltpu.make_async_copy(wa, A.at[me], own_sem.at[0]),
        pltpu.make_async_copy(wb, B.at[me], own_sem.at[1]),
    ]
    for copy in own:
        copy.start()
    blank = jnp.zeros((128, 128), BF16)
    E1[me] = blank
    E2[me] = blank
    E1[me, 0:100, :] = enc_in[...]
    E2[me, :, 0:100] = enc_out[...]

    @pl.when(x == 3)
    def _():
        C1[me] = blank
        C1[me, 0:100, 0:64] = conn_in[...]
        C2[me] = conn_out[...]

    pl.semaphore_wait(barrier, 7)

    def relay(groups, send, recv):
        first_of = (0, len(groups[0]))
        sent = [0, 0]
        pending = []
        steps = []
        y_at = (y, up(y, -1, 4), up(y, 1, 4), up(y, 2, 4))

        def copies(t, dz, i, number, to):
            slot = up(z, dz, 8) * 4 + y_at[i]
            return [
                remote(
                    part(slot), part(slot),
                    send.at[first_of[t] + e, number], recv.at[first_of[t] + e, slot], to,
                )
                for e, part in enumerate(groups[t])
            ]

        def go(t, dz, i, *tos):
            for to in tos:
                for copy in copies(t, dz, i, sent[t], to):
                    copy.start()
                    pending.append(copy)
                sent[t] += 1

        def came(t, dz, i, *tos):
            def step():
                for copy in copies(t, dz, i, 0, y_up):
                    copy.wait_recv()
                go(t, dz, i, *tos)

            steps.append(step)

        def across(place):
            dz = (0, -1, 1, -2, 2, -3, 3, 4)[place]
            came(1, dz, 1, *((y_up,) if place % 2 == 0 else ()))
            came(1, dz, 2, *((y_down,) if place % 2 == 1 else ()))

        def start():
            go(0, 0, 0, z_up, z_down, y_up, y_down)
            go(1, 0, 0, y_up, y_down, z_up, z_down)

        came(0, 0, 1, y_up, z_up, z_down)
        came(0, 0, 2, z_up, z_down)
        for r in (1, 2, 3):
            came(1, -r, 0, *((z_up,) if r < 3 else ()), y_up, y_down)
            came(1, r, 0, z_down, y_up, y_down)
            if r == 1:
                across(0)
                came(0, 0, 3, z_up, z_down)
            for i in range(4):
                came(0, -r, i, *((z_up,) if r < 3 or i % 2 == 0 else ()))
                came(0, r, i, *((z_down,) if r < 3 or i % 2 == 1 else ()))
                if r > 1 and i == 1:
                    across(2 * r - 3)
            if r > 1:
                across(2 * r - 2)
        came(1, 4, 0, y_up, y_down)
        for place in (5, 6, 7):
            across(place)
        for i in range(4):
            came(0, 4, i)
        for dz in (0, -1, 1, -2, 2, -3, 3, 4):
            came(1, dz, 3)

        def finish():
            for copy in pending:
                copy.wait_send()

        return start, steps, finish

    def exchange(mine, theirs, ssem, rsem, slot):
        copy = remote(mine, theirs, ssem.at[slot], rsem.at[slot], other)
        copy.start()
        copy.wait()
        return mine[...] + theirs[...]

    enc_start, enc_steps, enc_finish = relay(
        ((lambda s: E1.at[s],), (lambda s: E2.at[s],)), send_enc, recv_enc
    )
    llm_start, llm_steps, llm_finish = relay(
        (
            (lambda s: A.at[s, pl.ds(0, SPLIT)],),
            (lambda s: B.at[s], lambda s: A.at[s, pl.ds(SPLIT, 256 - SPLIT)]),
        ),
        send_llm, recv_llm,
    )
    enc_start()
    for copy in own:
        copy.wait()
    llm_start()

    def text_local(j):
        return pltpu.make_async_copy(
            text.at[:, pl.ds(pl.multiple_of(j * 512 + c * 256, 256), 256)],
            h0.at[c, :, pl.ds(j * 256, 256)],
            text_l.at[j],
        )

    def text_other(j):
        return remote(
            text.at[:, pl.ds(pl.multiple_of(j * 512 + o * 256, 256), 256)],
            h0.at[c, :, pl.ds(j * 256, 256)],
            text_s.at[j], text_r.at[j], other,
        )

    def text_came(j):
        return remote(
            text.at[:, pl.ds(0, 256)],
            h0.at[o, :, pl.ds(j * 256, 256)],
            text_s.at[j], text_r.at[j], other,
        )

    own_rows = pl.ds(pl.multiple_of(c * 48, 16), 48)
    other_rows = pl.ds(pl.multiple_of(o * 48, 16), 48)
    image_other = remote(img2.at[o], henc.at[own_rows], misc_s.at[0], misc_r.at[0], other)
    marks_other = remote(ohb.at[c], ohb.at[c], misc_s.at[1], misc_r.at[1], other)

    @pl.when(x == 0)
    def _():
        spread = lax.broadcasted_iota(jnp.int32, (256, 128), 0)
        lane = lax.broadcasted_iota(jnp.int32, (256, 128), 1)
        for b in range(2 * BLOCKS):
            base = 100 * b // 128 * 128
            width = min(256, 3200 - base)
            pick = (spread == lane + (100 * b - base)) & (lane < 100)
            pick = jnp.where(pick, 1.0, 0.0).astype(BF16)[0:width]
            block = matmul(image[:, base : base + width], pick).astype(BF16)
            img2[b % 2, :, b // 2 * 128 : (b // 2 + 1) * 128] = block
        image_other.start()
        henc[own_rows, :] = img2[c]
        spot = jnp.full((1, 128), -1.0, F32)
        for m in range(3):
            j = lax.broadcasted_iota(jnp.int32, (16, 128), 0)
            at = lax.broadcasted_iota(jnp.int32, (16, 128), 1)
            pick = jnp.where(at == j + (m * 16 + c * 48), 1.0, 0.0).astype(BF16)
            rows = (positions[m : m + 1, :] + (64 * m + 1)).astype(F32).astype(BF16)
            spot += matmul(jnp.broadcast_to(rows, (16, 16)), pick)[0:1]
        row = lax.broadcasted_iota(jnp.int32, (192, 128), 0).astype(F32)
        ohb[c] = jnp.where(row == spot, 1.0, 0.0).astype(BF16)
        marks_other.start()
        for j in range(BLOCKS):
            text_local(j).start()
            text_other(j).start()

    for step in enc_steps:
        step()
    enc_finish()

    conn_start, conn_steps, conn_finish = relay(
        ((lambda s: C1.at[s],), (lambda s: C2.at[s],)), send_enc, recv_conn
    )

    @pl.when(x == 3)
    def _():
        conn_start()
        for step in conn_steps:
            step()
        conn_finish()

    def projected(slot, weight):
        h = henc[...]
        es[slot, :, 0:128] = matmul(h, weight.reshape(BLOCKS * 128, 128))
        squares = jnp.zeros((96, 128), F32)
        for j in range(BLOCKS):
            part = h[:, j * 128 : (j + 1) * 128].astype(F32)
            squares += part * part
        es[slot, :, 128:256] = squares
        total = exchange(es.at[slot], er.at[slot], xe_s, xe_r, slot)
        scale = lax.rsqrt(
            jnp.sum(total[:, 128:256], axis=-1, keepdims=True) * (1.0 / 3200) + EPSILON
        )
        return gelu(total[:, 0:128] * scale).astype(BF16)

    passed = remote(henc, henc, misc_s.at[2], misc_r.at[2], x_next)
    pictures = remote(
        imgrows.at[pl.ds(0, 96)], imgrows.at[pl.ds(0, 96)], misc_s.at[3], misc_r.at[3], x_next
    )

    def encoder(plane):
        @pl.when(x == plane)
        def _():
            if plane == 0:
                image_other.wait_send()
                remote(
                    img2.at[c], henc.at[other_rows], misc_s.at[0], misc_r.at[0], other
                ).wait_recv()
            else:
                passed.wait_recv()

            def layer(l, _):
                activated = projected(l, E1[pl.ds(l * BLOCKS, BLOCKS)])
                for j in range(BLOCKS):
                    branch = matmul(activated, E2[l * BLOCKS + j])
                    span = slice(j * 128, (j + 1) * 128)
                    henc[:, span] = (henc[:, span].astype(F32) + branch).astype(BF16)
                return 0

            lax.fori_loop(0, 2, layer, 0)
            if plane < 3:
                passed.start()
            else:
                latent = projected(0, C1[0:BLOCKS])[:, 0:64]
                for j in range(BLOCKS):
                    imgrows[0:96, j * 256 : (j + 1) * 256] = matmul(latent, C2[j]).astype(BF16)
                pictures.start()

    encoder(0)
    turns = {int(len(llm_steps) * part): plane for plane, part in TURNS}
    for number, step in enumerate(llm_steps):
        if number in turns:
            encoder(turns[number])
        step()
    llm_finish()

    @pl.when(x == 0)
    def _():
        marks_other.wait_send()
        remote(ohb.at[o], ohb.at[o], misc_s.at[1], misc_r.at[1], other).wait_recv()
        for j in range(BLOCKS):
            text_local(j).wait()
            text_other(j).wait_send()
            text_came(j).wait_recv()
        imgrows[96:128, :] = jnp.zeros((32, BLOCKS * 256), BF16)
        pictures.wait_recv()

    @pl.when(x == 3)
    def _():
        pictures.wait_send()

    @pl.when(x < 3)
    def _():
        passed.wait_send()

    def cols(j):
        return slice(j * 256, (j + 1) * 256)

    def folded(v):
        return v[:, 0:128] * v[:, 0:128] + v[:, 128:256] * v[:, 128:256]

    def activation(slot, size, acc, squares):
        mine = xs.at[slot, pl.ds(0, size)]
        mine[:, 0:512] = acc
        mine[:, 512:640] = squares
        total = exchange(mine, xr.at[slot, pl.ds(0, size)], x_s, x_r, slot)
        scale = lax.rsqrt(
            jnp.sum(total[:, 512:640], axis=-1, keepdims=True) * (1.0 / 8192) + EPSILON
        )
        return silu(total[:, 0:512] * scale).astype(BF16)

    def chunk(k, start, count, merge_last):
        size = 2 * count
        base = pl.multiple_of(2 * start, size)
        rows = pl.ds(pl.multiple_of(start, count), count)
        both = pl.ds(base, size)
        mine = pl.ds(pl.multiple_of(base + c * count, count), count)
        theirs = pl.ds(pl.multiple_of(base + o * count, count), count)

        def flow(part):
            span = hin.at[both, pl.ds(part * 1024, 1024)]
            return remote(span, span, flow_s.at[k, part], flow_r.at[k, part], x_next)

        def emit():
            for j in range(BLOCKS):
                out[rows, pl.ds(pl.multiple_of(j * 512 + c * 256, 256), 256)] = hin[mine, cols(j)]
            osend[rows, :] = hin[theirs, :]
            result(k, start, count).start()

        @pl.when(x == 0)
        def _():
            marks = jnp.concatenate([ohb[0, rows, :], ohb[1, rows, :]], axis=0)
            hit = jnp.sum(marks.astype(F32), axis=-1, keepdims=True) > 0.5
            for j in range(BLOCKS):
                placed = matmul(marks, imgrows[:, cols(j)])
                words = jnp.concatenate([h0[0, rows, cols(j)], h0[1, rows, cols(j)]], axis=0)
                hin[both, cols(j)] = jnp.where(hit, placed, words.astype(F32)).astype(BF16)

        acc, squares = jnp.zeros((size, 512), F32), jnp.zeros((size, 128), F32)
        for part in range(4):

            @pl.when(x > 0)
            def _():
                flow(part).wait_recv()

            for j in range(4 * part, 4 * part + 4):
                h = hin[both, cols(j)]
                acc, squares = acc + matmul(h, A[j]), squares + folded(h.astype(F32))
        a = activation(0, size, acc, squares)
        acc, squares = jnp.zeros((size, 512), F32), jnp.zeros((size, 128), F32)
        for j in range(BLOCKS):
            h = (hin[both, cols(j)].astype(F32) + matmul(a, B[j])).astype(BF16)
            hin[both, cols(j)] = h
            acc, squares = acc + matmul(h, A[BLOCKS + j]), squares + folded(h.astype(F32))

        @pl.when(z_hi == 0)
        def _():
            emit()

        b = activation(1, size, acc, squares)
        for part in range(4):
            for j in range(4 * part, 4 * part + 4):
                h = hin[both, cols(j)].astype(F32) + matmul(b, B[BLOCKS + j])
                hin[both, cols(j)] = h.astype(BF16)

            @pl.when(x < 3)
            def _():
                flow(part).start()

        @pl.when(z_hi == 1)
        def _():
            emit()

        merge_last()

        def drain():
            result(k, start, count).wait_send()

            @pl.when(x < 3)
            def _():
                for part in range(4):
                    flow(part).wait_send()

        return drain

    def result(k, start, count):
        rows = pl.ds(pl.multiple_of(start, count), count)
        return remote(osend.at[rows], orecv.at[rows], out_s.at[k], out_r.at[k], other)

    def merge(k, start, count):
        result(k, start, count).wait_recv()
        rows = pl.ds(pl.multiple_of(start, count), count)
        for j in range(BLOCKS):
            out[rows, pl.ds(pl.multiple_of(j * 512 + o * 256, 256), 256)] = orecv[rows, cols(j)]

    def full(k, _):
        def merge_last():
            @pl.when(k > 0)
            def _():
                merge(k - 1, (k - 1) * 32, 32)

        chunk(k, k * 32, 32, merge_last)
        return 0

    lax.fori_loop(0, 5, full, 0)
    half = [
        chunk(5, 160, 16, lambda: merge(4, 128, 32)),
        chunk(6, 176, 16, lambda: merge(5, 160, 16)),
    ]
    merge(6, 176, 16)

    def drain(k, _):
        result(k, k * 32, 32).wait_send()

        @pl.when(x < 3)
        def _():
            for part in range(4):
                span = hin.at[
                    pl.ds(pl.multiple_of(k * 64, 64), 64), pl.ds(part * 1024, 1024)
                ]
                remote(span, span, flow_s.at[k, part], flow_r.at[k, part], x_next).wait_send()

        return 0

    lax.fori_loop(0, 5, drain, 0)
    for finish in half:
        finish()


def local(text, image, positions, enc_in, enc_out, conn_in, conn_out, llm_in, llm_out):
    any_spec = pl.BlockSpec(memory_space=pl.ANY)
    vmem_spec = pl.BlockSpec(memory_space=pltpu.VMEM)
    dma = pltpu.SemaphoreType.DMA
    hidden = pl.pallas_call(
        kernel,
        out_shape=jax.ShapeDtypeStruct((192, 8192), BF16),
        in_specs=[any_spec] + [vmem_spec] * 6 + [any_spec] * 2,
        out_specs=vmem_spec,
        scratch_shapes=[
            pltpu.VMEM((32, 256, 512), BF16),
            pltpu.VMEM((32, 512, 256), BF16),
            pltpu.VMEM((32, 128, 128), BF16),
            pltpu.VMEM((32, 128, 128), BF16),
            pltpu.VMEM((32, 128, 128), BF16),
            pltpu.VMEM((32, 64, 256), BF16),
            pltpu.VMEM((2, 192, 4096), BF16),
            pltpu.VMEM((2, 192, 128), BF16),
            pltpu.VMEM((2, 48, 2048), BF16),
            pltpu.VMEM((96, 2048), BF16),
            pltpu.VMEM((128, 4096), BF16),
            pltpu.VMEM((2, 64, 640), F32),
            pltpu.VMEM((2, 64, 640), F32),
            pltpu.VMEM((2, 96, 256), F32),
            pltpu.VMEM((2, 96, 256), F32),
            pltpu.VMEM((384, 4096), BF16),
            pltpu.VMEM((192, 4096), BF16),
            pltpu.VMEM((192, 4096), BF16),
            dma((3, 31)),
            dma((3, 32)),
            dma((2, 31)),
            dma((2, 32)),
            dma((2, 32)),
            dma((2,)),
            dma((16,)),
            dma((16,)),
            dma((16,)),
            dma((4,)),
            dma((4,)),
            dma((2,)),
            dma((2,)),
            dma((2,)),
            dma((2,)),
            dma((7, 4)),
            dma((7, 4)),
            dma((7,)),
            dma((7,)),
        ],
        compiler_params=pltpu.CompilerParams(
            collective_id=0, has_side_effects=True, vmem_limit_bytes=60 * 1024 * 1024
        ),
        cost_estimate=pl.CostEstimate(
            flops=14_000_000_000, bytes_accessed=16_000_000, transcendentals=1_000_000
        ),
    )(text, image, positions, enc_in[0], enc_out[0], conn_in, conn_out, llm_in[0], llm_out[0])
    return hidden[None]


def solution(mesh):
    return jax.shard_map(
        local,
        mesh=mesh,
        in_specs=(
            P("dp", None),
            P("dp", None),
            P("dp", None),
            P("section", "dp", None),
            P("section", None, "dp"),
            P("dp", None),
            P(None, "dp"),
            P("section", "dp", None),
            P("section", None, "dp"),
        ),
        out_specs=P("section", "dp", None),
        check_vma=False,
    )
```

```python
import jax
import jax.numpy as jnp
from jax import lax
from jax.experimental import pallas as pl
from jax.experimental.pallas import tpu as pltpu
from jax.sharding import PartitionSpec as P

EPSILON = 1e-06
MESH = pl.DeviceIdType.MESH
F32 = jnp.float32
BF16 = jnp.bfloat16
SPLIT = 192
TURN = 8
BLOCKS = 16


def gelu(v):
    return 0.5 * v * (1.0 + lax.erf(v * 0.7071067811865476))


def silu(v):
    return v / (1.0 + jnp.exp(-v))


def matmul(a, b):
    return jnp.dot(a, b, preferred_element_type=F32)


def device(x, y, z, c):
    return (x * 2 + z // 4, lax.rem(z, 4) * 8 + y * 2 + c)


def kernel(
    text, image, positions, enc_in, enc_out, conn_in, conn_out, wa, wb, out,
    A, B, E1, E2, C1, C2, ep, h0, ohb, img2, henc, imgrows, xs, xr, es, er, hin, osend, orecv,
    send_llm, recv_llm, send_enc, recv_enc, gather_s, gather_r, own_sem, text_l, text_s, text_r,
    misc_s, misc_r, x_s, x_r, xe_s, xe_r, flow_s, flow_r, out_s, out_r,
):
    section = lax.axis_index("section")
    dp = lax.axis_index("dp")
    x, z_hi = section // 2, lax.rem(section, 2)
    z = z_hi * 4 + dp // 8
    y = lax.rem(dp // 2, 4)
    c = lax.rem(dp, 2)
    o = 1 - c
    me = z * 4 + y

    def up(v, by, n):
        return lax.rem(v + by + n, n)

    y_up, y_down = device(x, up(y, 1, 4), z, c), device(x, up(y, -1, 4), z, c)
    z_up, z_down = device(x, y, up(z, 1, 8), c), device(x, y, up(z, -1, 8), c)
    other = device(x, y, z, o)
    x_next = device(up(x, 1, 4), y, z, c)
    x_last = device(up(x, -1, 4), y, z, c)

    def remote(src, dst, ssem, rsem, to):
        return pltpu.make_async_remote_copy(
            src_ref=src, dst_ref=dst, send_sem=ssem, recv_sem=rsem, device_id=to, device_id_type=MESH
        )

    barrier = pltpu.get_barrier_semaphore()
    for to in (y_up, y_down, z_up, z_down, other, x_next, x_last, device(up(x, 2, 4), y, z, c)):
        pl.semaphore_signal(barrier, inc=1, device_id=to, device_id_type=MESH)

    own = [
        pltpu.make_async_copy(wa, A.at[me], own_sem.at[0]),
        pltpu.make_async_copy(wb, B.at[me], own_sem.at[1]),
    ]
    for copy in own:
        copy.start()
    blank = jnp.zeros((128, 128), BF16)
    ep[0] = blank
    ep[1] = blank
    ep[0, 0:100, :] = enc_in[...]
    ep[1, :, 0:100] = enc_out[...]

    @pl.when(x == 3)
    def _():
        C1[me] = blank
        C1[me, 0:100, 0:64] = conn_in[...]
        C2[me] = conn_out[...]
        E1[me, 1] = ep[0]
        E2[me, 1] = ep[1]

    pl.semaphore_wait(barrier, 8)

    def gathered(source):
        to = device(max(2, source + 1), y, z, c)
        k = source % 2
        return [
            remote(ep.at[e], place.at[me, k], gather_s.at[e], gather_r.at[e, k], to)
            for e, place in ((0, E1), (1, E2))
        ]

    for source in range(3):

        @pl.when(x == source)
        def _():
            for copy in gathered(source):
                copy.start()

    def relay(groups, send, recv):
        first_of = (0, len(groups[0]))
        sent = [0, 0]
        pending = []
        steps = []
        y_at = (y, up(y, -1, 4), up(y, 1, 4), up(y, 2, 4))

        def copies(t, dz, i, number, to):
            slot = up(z, dz, 8) * 4 + y_at[i]
            return [
                remote(
                    part(slot), part(slot),
                    send.at[first_of[t] + e, number], recv.at[first_of[t] + e, slot], to,
                )
                for e, part in enumerate(groups[t])
            ]

        def go(t, dz, i, *tos):
            for to in tos:
                for copy in copies(t, dz, i, sent[t], to):
                    copy.start()
                    pending.append(copy)
                sent[t] += 1

        def came(t, dz, i, *tos):
            def step():
                for copy in copies(t, dz, i, 0, y_up):
                    copy.wait_recv()
                go(t, dz, i, *tos)

            steps.append(step)

        def across(place):
            dz = (0, -1, 1, -2, 2, -3, 3, 4)[place]
            came(1, dz, 1, *((y_up,) if place % 2 == 0 else ()))
            came(1, dz, 2, *((y_down,) if place % 2 == 1 else ()))

        def start():
            go(1, 0, 0, z_up, z_down)
            go(0, 0, 0, y_up, y_down, z_up, z_down)
            go(1, 0, 0, y_up, y_down)

        came(0, 0, 1, y_up, z_up, z_down)
        came(0, 0, 2, z_up, z_down)
        came(1, -1, 0, z_up, y_up, y_down)
        came(1, 1, 0, z_down, y_up, y_down)
        came(0, 0, 3, z_up, z_down)
        across(0)
        came(0, -1, 0, z_up)
        came(0, 1, 0, z_down)
        came(1, -2, 0, z_up, y_up, y_down)
        came(1, 2, 0, z_down, y_up, y_down)
        came(0, -1, 1, z_up)
        came(0, 1, 1, z_down)
        across(1)
        came(0, -1, 2, z_up)
        came(0, 1, 2, z_down)
        came(1, -3, 0, y_up, y_down)
        came(1, 3, 0, z_down, y_up, y_down)
        across(2)
        came(0, -1, 3, z_up)
        came(0, 1, 3, z_down)
        came(0, -2, 0, z_up)
        came(0, 2, 0, z_down)
        across(3)
        came(1, 4, 0, y_up, y_down)
        came(0, -2, 1, z_up)
        came(0, 2, 1, z_down)
        across(4)
        came(0, -2, 2, z_up)
        came(0, 2, 2, z_down)
        across(5)
        came(0, -2, 3, z_up)
        came(0, 2, 3, z_down)
        came(0, -3, 0, z_up)
        came(0, 3, 0)
        across(6)
        came(0, -3, 1)
        came(0, 3, 1, z_down)
        came(0, -3, 2, z_up)
        came(0, 3, 2)
        across(7)
        came(0, -3, 3)
        came(0, 3, 3, z_down)
        for i in range(4):
            came(0, 4, i)
        for dz in (0, -1, 1, -2, 2, -3, 3, 4):
            came(1, dz, 3)

        def finish():
            for copy in pending:
                copy.wait_send()

        return start, steps, finish

    def exchange(mine, theirs, ssem, rsem, slot):
        copy = remote(mine, theirs, ssem.at[slot], rsem.at[slot], other)
        copy.start()
        copy.wait()
        return mine[...] + theirs[...]

    llm_start, llm_steps, llm_finish = relay(
        (
            (lambda s: A.at[s, pl.ds(0, SPLIT)],),
            (lambda s: B.at[s], lambda s: A.at[s, pl.ds(SPLIT, 256 - SPLIT)]),
        ),
        send_llm, recv_llm,
    )
    for copy in own:
        copy.wait()

    own_rows = pl.ds(pl.multiple_of(c * 48, 16), 48)
    other_rows = pl.ds(pl.multiple_of(o * 48, 16), 48)
    image_other = remote(img2.at[o], henc.at[own_rows], misc_s.at[0], misc_r.at[0], other)

    @pl.when(x == 2)
    def _():
        spread = lax.broadcasted_iota(jnp.int32, (256, 128), 0)
        lane = lax.broadcasted_iota(jnp.int32, (256, 128), 1)
        for b in range(2 * BLOCKS):
            base = 100 * b // 128 * 128
            width = min(256, 3200 - base)
            pick = (spread == lane + (100 * b - base)) & (lane < 100)
            pick = jnp.where(pick, 1.0, 0.0).astype(BF16)[0:width]
            block = matmul(image[:, base : base + width], pick).astype(BF16)
            img2[b % 2, :, b // 2 * 128 : (b // 2 + 1) * 128] = block
        image_other.start()
        henc[own_rows, :] = img2[c]

    @pl.when(x == 2)
    def _():
        for source in (0, 1):
            for copy in gathered(source):
                copy.wait_recv()
        start, steps, finish = relay(
            ((lambda s: E1.at[s],), (lambda s: E2.at[s],)), send_enc, recv_enc
        )
        start()
        for step in steps:
            step()
        finish()

    @pl.when(x == 3)
    def _():
        for copy in gathered(2):
            copy.wait_recv()
        start, steps, finish = relay(
            (
                (lambda s: E1.at[s], lambda s: C1.at[s]),
                (lambda s: E2.at[s], lambda s: C2.at[s]),
            ),
            send_enc, recv_enc,
        )
        start()
        for step in steps:
            step()
        finish()

    llm_start()

    def text_local(j):
        return pltpu.make_async_copy(
            text.at[:, pl.ds(pl.multiple_of(j * 512 + c * 256, 256), 256)],
            h0.at[c, :, pl.ds(j * 256, 256)],
            text_l.at[j],
        )

    def text_other(j):
        return remote(
            text.at[:, pl.ds(pl.multiple_of(j * 512 + o * 256, 256), 256)],
            h0.at[c, :, pl.ds(j * 256, 256)],
            text_s.at[j], text_r.at[j], other,
        )

    def text_came(j):
        return remote(
            text.at[:, pl.ds(0, 256)],
            h0.at[o, :, pl.ds(j * 256, 256)],
            text_s.at[j], text_r.at[j], other,
        )

    marks_other = remote(ohb.at[c], ohb.at[c], misc_s.at[1], misc_r.at[1], other)

    @pl.when(x == 0)
    def _():
        spot = jnp.full((1, 128), -1.0, F32)
        for m in range(3):
            j = lax.broadcasted_iota(jnp.int32, (16, 128), 0)
            at = lax.broadcasted_iota(jnp.int32, (16, 128), 1)
            pick = jnp.where(at == j + (m * 16 + c * 48), 1.0, 0.0).astype(BF16)
            rows = (positions[m : m + 1, :] + (64 * m + 1)).astype(F32).astype(BF16)
            spot += matmul(jnp.broadcast_to(rows, (16, 16)), pick)[0:1]
        row = lax.broadcasted_iota(jnp.int32, (192, 128), 0).astype(F32)
        ohb[c] = jnp.where(row == spot, 1.0, 0.0).astype(BF16)
        marks_other.start()
        for j in range(BLOCKS):
            text_local(j).start()
            text_other(j).start()

    def projected(slot, weight):
        h = henc[...]
        es[slot, :, 0:128] = matmul(h, weight.reshape(BLOCKS * 128, 128))
        squares = jnp.zeros((96, 128), F32)
        for j in range(BLOCKS):
            part = h[:, j * 128 : (j + 1) * 128].astype(F32)
            squares += part * part
        es[slot, :, 128:256] = squares
        total = exchange(es.at[slot], er.at[slot], xe_s, xe_r, slot)
        scale = lax.rsqrt(
            jnp.sum(total[:, 128:256], axis=-1, keepdims=True) * (1.0 / 3200) + EPSILON
        )
        return gelu(total[:, 0:128] * scale).astype(BF16)

    passed = remote(henc, henc, misc_s.at[2], misc_r.at[2], x_next)
    pictures = remote(
        imgrows.at[pl.ds(0, 96)], imgrows.at[pl.ds(0, 96)], misc_s.at[3], misc_r.at[3], x_next
    )

    def encoder(plane):
        @pl.when(x == plane)
        def _():
            if plane == 2:
                image_other.wait_send()
                remote(
                    img2.at[c], henc.at[other_rows], misc_s.at[0], misc_r.at[0], other
                ).wait_recv()
            else:
                passed.wait_recv()

            def layer(l, _):
                k, half = l // 2, lax.rem(l, 2)
                activated = projected(half, E1[pl.ds(half * BLOCKS, BLOCKS), k])
                for j in range(BLOCKS):
                    branch = matmul(activated, E2[half * BLOCKS + j, k])
                    span = slice(j * 128, (j + 1) * 128)
                    henc[:, span] = (henc[:, span].astype(F32) + branch).astype(BF16)
                return 0

            lax.fori_loop(0, 4, layer, 0)
            if plane == 2:
                passed.start()
            else:
                latent = projected(0, C1[0:BLOCKS])[:, 0:64]
                for j in range(BLOCKS):
                    imgrows[0:96, j * 256 : (j + 1) * 256] = matmul(latent, C2[j]).astype(BF16)
                pictures.start()

    encoder(2)
    for number, step in enumerate(llm_steps):
        if number == TURN:
            encoder(3)
        step()
    llm_finish()

    @pl.when(x == 0)
    def _():
        marks_other.wait_send()
        remote(ohb.at[o], ohb.at[o], misc_s.at[1], misc_r.at[1], other).wait_recv()
        for j in range(BLOCKS):
            text_local(j).wait()
            text_other(j).wait_send()
            text_came(j).wait_recv()
        imgrows[96:128, :] = jnp.zeros((32, BLOCKS * 256), BF16)
        pictures.wait_recv()

    @pl.when(x == 3)
    def _():
        pictures.wait_send()

    @pl.when(x == 2)
    def _():
        passed.wait_send()

    for source in range(3):

        @pl.when(x == source)
        def _():
            for copy in gathered(source):
                copy.wait_send()

    def cols(j):
        return slice(j * 256, (j + 1) * 256)

    def folded(v):
        return v[:, 0:128] * v[:, 0:128] + v[:, 128:256] * v[:, 128:256]

    def activation(slot, size, acc, squares):
        mine = xs.at[slot, pl.ds(0, size)]
        mine[:, 0:512] = acc
        mine[:, 512:640] = squares
        total = exchange(mine, xr.at[slot, pl.ds(0, size)], x_s, x_r, slot)
        scale = lax.rsqrt(
            jnp.sum(total[:, 512:640], axis=-1, keepdims=True) * (1.0 / 8192) + EPSILON
        )
        return silu(total[:, 0:512] * scale).astype(BF16)

    def flow(k, start, count, part):
        base = pl.multiple_of(2 * start, 2 * count)
        span = hin.at[pl.ds(base, 2 * count), pl.ds(part * 1024, 1024)]
        return remote(span, span, flow_s.at[k, part], flow_r.at[k, part], x_next)

    def chunk(k, start, count, merge_last, sent_last):
        size = 2 * count
        base = pl.multiple_of(2 * start, size)
        rows = pl.ds(pl.multiple_of(start, count), count)
        both = pl.ds(base, size)
        mine = pl.ds(pl.multiple_of(base + c * count, count), count)
        theirs = pl.ds(pl.multiple_of(base + o * count, count), count)

        def emit():
            for j in range(BLOCKS):
                out[rows, pl.ds(pl.multiple_of(j * 512 + c * 256, 256), 256)] = hin[mine, cols(j)]
            osend[rows, :] = hin[theirs, :]
            result(k, start, count).start()

        @pl.when(x == 0)
        def _():
            marks = jnp.concatenate([ohb[0, rows, :], ohb[1, rows, :]], axis=0)
            hit = jnp.sum(marks.astype(F32), axis=-1, keepdims=True) > 0.5
            for j in range(BLOCKS):
                placed = matmul(marks, imgrows[:, cols(j)])
                words = jnp.concatenate([h0[0, rows, cols(j)], h0[1, rows, cols(j)]], axis=0)
                hin[both, cols(j)] = jnp.where(hit, placed, words.astype(F32)).astype(BF16)

        acc, squares = jnp.zeros((size, 512), F32), jnp.zeros((size, 128), F32)
        for part in range(4):

            @pl.when(x > 0)
            def _():
                flow(k, start, count, part).wait_recv()

            for j in range(4 * part, 4 * part + 4):
                h = hin[both, cols(j)]
                acc, squares = acc + matmul(h, A[j]), squares + folded(h.astype(F32))
        a = activation(0, size, acc, squares)
        acc, squares = jnp.zeros((size, 512), F32), jnp.zeros((size, 128), F32)
        for j in range(BLOCKS):
            h = (hin[both, cols(j)].astype(F32) + matmul(a, B[j])).astype(BF16)
            hin[both, cols(j)] = h
            acc, squares = acc + matmul(h, A[BLOCKS + j]), squares + folded(h.astype(F32))

        @pl.when(z_hi == 0)
        def _():
            emit()

        b = activation(1, size, acc, squares)
        for part in range(4):
            for j in range(4 * part, 4 * part + 4):
                h = hin[both, cols(j)].astype(F32) + matmul(b, B[BLOCKS + j])
                hin[both, cols(j)] = h.astype(BF16)

            @pl.when(x < 3)
            def _():
                sent_last(part)
                flow(k, start, count, part).start()

        @pl.when(z_hi == 1)
        def _():
            emit()

        merge_last()

    def result(k, start, count):
        rows = pl.ds(pl.multiple_of(start, count), count)
        return remote(osend.at[rows], orecv.at[rows], out_s.at[k], out_r.at[k], other)

    def merge(k, start, count):
        result(k, start, count).wait_recv()
        rows = pl.ds(pl.multiple_of(start, count), count)
        for j in range(BLOCKS):
            out[rows, pl.ds(pl.multiple_of(j * 512 + o * 256, 256), 256)] = orecv[rows, cols(j)]

    def full(k, _):
        def merge_last():
            @pl.when(k > 0)
            def _():
                merge(k - 1, (k - 1) * 32, 32)

        def sent_last(part):
            @pl.when(k > 0)
            def _():
                flow(k - 1, (k - 1) * 32, 32, part).wait_send()

        chunk(k, k * 32, 32, merge_last, sent_last)
        return 0

    lax.fori_loop(0, 5, full, 0)
    chunk(
        5, 160, 16,
        lambda: merge(4, 128, 32),
        lambda part: flow(4, 128, 32, part).wait_send(),
    )
    chunk(
        6, 176, 16,
        lambda: merge(5, 160, 16),
        lambda part: flow(5, 160, 16, part).wait_send(),
    )
    merge(6, 176, 16)

    def drain(k, _):
        result(k, k * 32, 32).wait_send()
        return 0

    lax.fori_loop(0, 5, drain, 0)
    result(5, 160, 16).wait_send()
    result(6, 176, 16).wait_send()

    @pl.when(x < 3)
    def _():
        for part in range(4):
            flow(6, 176, 16, part).wait_send()


def local(text, image, positions, enc_in, enc_out, conn_in, conn_out, llm_in, llm_out):
    any_spec = pl.BlockSpec(memory_space=pl.ANY)
    vmem_spec = pl.BlockSpec(memory_space=pltpu.VMEM)
    dma = pltpu.SemaphoreType.DMA
    hidden = pl.pallas_call(
        kernel,
        out_shape=jax.ShapeDtypeStruct((192, 8192), BF16),
        in_specs=[any_spec] + [vmem_spec] * 6 + [any_spec] * 2,
        out_specs=vmem_spec,
        scratch_shapes=[
            pltpu.VMEM((32, 256, 512), BF16),
            pltpu.VMEM((32, 512, 256), BF16),
            pltpu.VMEM((32, 2, 128, 128), BF16),
            pltpu.VMEM((32, 2, 128, 128), BF16),
            pltpu.VMEM((32, 128, 128), BF16),
            pltpu.VMEM((32, 64, 256), BF16),
            pltpu.VMEM((2, 128, 128), BF16),
            pltpu.VMEM((2, 192, 4096), BF16),
            pltpu.VMEM((2, 192, 128), BF16),
            pltpu.VMEM((2, 48, 2048), BF16),
            pltpu.VMEM((96, 2048), BF16),
            pltpu.VMEM((128, 4096), BF16),
            pltpu.VMEM((2, 64, 640), F32),
            pltpu.VMEM((2, 64, 640), F32),
            pltpu.VMEM((2, 96, 256), F32),
            pltpu.VMEM((2, 96, 256), F32),
            pltpu.VMEM((384, 4096), BF16),
            pltpu.VMEM((192, 4096), BF16),
            pltpu.VMEM((192, 4096), BF16),
            dma((3, 31)),
            dma((3, 32)),
            dma((4, 31)),
            dma((4, 32)),
            dma((2,)),
            dma((2, 2)),
            dma((2,)),
            dma((16,)),
            dma((16,)),
            dma((16,)),
            dma((4,)),
            dma((4,)),
            dma((2,)),
            dma((2,)),
            dma((2,)),
            dma((2,)),
            dma((7, 4)),
            dma((7, 4)),
            dma((7,)),
            dma((7,)),
        ],
        compiler_params=pltpu.CompilerParams(
            collective_id=0, has_side_effects=True, vmem_limit_bytes=60 * 1024 * 1024
        ),
        cost_estimate=pl.CostEstimate(
            flops=14_000_000_000, bytes_accessed=16_000_000, transcendentals=1_000_000
        ),
    )(text, image, positions, enc_in[0], enc_out[0], conn_in, conn_out, llm_in[0], llm_out[0])
    return hidden[None]


def solution(mesh):
    return jax.shard_map(
        local,
        mesh=mesh,
        in_specs=(
            P("dp", None),
            P("dp", None),
            P("dp", None),
            P("section", "dp", None),
            P("section", None, "dp"),
            P("dp", None),
            P(None, "dp"),
            P("section", "dp", None),
            P("section", None, "dp"),
        ),
        out_specs=P("section", "dp", None),
        check_vma=False,
    )
```

```python
import jax
import jax.numpy as jnp
from jax import lax
from jax.experimental import pallas as pl
from jax.experimental.pallas import tpu as pltpu
from jax.sharding import PartitionSpec as P

EPSILON = 1e-06
MESH = pl.DeviceIdType.MESH
F32 = jnp.float32
BF16 = jnp.bfloat16
SPLIT = 192
TURN = 8
BLOCKS = 16


def gelu(v):
    return 0.5 * v * (1.0 + lax.erf(v * 0.7071067811865476))


def silu(v):
    return v / (1.0 + jnp.exp(-v))


def matmul(a, b):
    return jnp.dot(a, b, preferred_element_type=F32)


def device(x, y, z, c):
    return (x * 2 + z // 4, lax.rem(z, 4) * 8 + y * 2 + c)


def kernel(
    text, image, positions, enc_in, enc_out, conn_in, conn_out, wa, wb, out,
    A, B, E1, E2, C1, C2, ep, h0, ohb, img2, henc, imgrows, xs, xr, es, er, hin, osend, orecv,
    zout, zin,
    send_llm, recv_llm, send_enc, recv_enc, gather_s, gather_r, own_sem, text_l, text_s, text_r,
    misc_s, misc_r, x_s, x_r, xe_s, xe_r, flow_s, flow_r, out_s, out_r, z_s, z_r,
):
    section = lax.axis_index("section")
    dp = lax.axis_index("dp")
    x, z_hi = section // 2, lax.rem(section, 2)
    z = z_hi * 4 + dp // 8
    y = lax.rem(dp // 2, 4)
    c = lax.rem(dp, 2)
    o = 1 - c
    me = z * 4 + y

    def up(v, by, n):
        return lax.rem(v + by + n, n)

    y_up, y_down = device(x, up(y, 1, 4), z, c), device(x, up(y, -1, 4), z, c)
    z_up, z_down = device(x, y, up(z, 1, 8), c), device(x, y, up(z, -1, 8), c)
    other = device(x, y, z, o)
    x_next = device(up(x, 1, 4), y, z, c)
    x_last = device(up(x, -1, 4), y, z, c)
    x_far = device(up(x, 2, 4), y, z, c)
    opposite = device(x, y, up(z, 4, 8), c)

    def remote(src, dst, ssem, rsem, to):
        return pltpu.make_async_remote_copy(
            src_ref=src, dst_ref=dst, send_sem=ssem, recv_sem=rsem, device_id=to, device_id_type=MESH
        )

    barrier = pltpu.get_barrier_semaphore()
    for to in (y_up, y_down, z_up, z_down, other, x_next, x_last, x_far, opposite):
        pl.semaphore_signal(barrier, inc=1, device_id=to, device_id_type=MESH)

    own = [
        pltpu.make_async_copy(wa, A.at[me], own_sem.at[0]),
        pltpu.make_async_copy(wb, B.at[me], own_sem.at[1]),
    ]
    for copy in own:
        copy.start()
    blank = jnp.zeros((128, 128), BF16)
    ep[0] = blank
    ep[1] = blank
    ep[0, 0:100, :] = enc_in[...]
    ep[1, :, 0:100] = enc_out[...]

    @pl.when(x == 3)
    def _():
        C1[me] = blank
        C1[me, 0:100, 0:64] = conn_in[...]
        C2[me] = conn_out[...]
        E1[me, 1] = ep[0]
        E2[me, 1] = ep[1]

    pl.semaphore_wait(barrier, 9)

    def gathered(source):
        to = device(max(2, source + 1), y, z, c)
        k = source % 2
        return [
            remote(ep.at[e], place.at[me, k], gather_s.at[e], gather_r.at[e, k], to)
            for e, place in ((0, E1), (1, E2))
        ]

    for source in range(3):

        @pl.when(x == source)
        def _():
            for copy in gathered(source):
                copy.start()

    def relay(groups, send, recv):
        first_of = (0, len(groups[0]))
        sent = [0, 0]
        pending = []
        steps = []
        y_at = (y, up(y, -1, 4), up(y, 1, 4), up(y, 2, 4))

        def copies(t, dz, i, number, to):
            slot = up(z, dz, 8) * 4 + y_at[i]
            return [
                remote(
                    part(slot), part(slot),
                    send.at[first_of[t] + e, number], recv.at[first_of[t] + e, slot], to,
                )
                for e, part in enumerate(groups[t])
            ]

        def go(t, dz, i, *tos):
            for to in tos:
                for copy in copies(t, dz, i, sent[t], to):
                    copy.start()
                    pending.append(copy)
                sent[t] += 1

        def came(t, dz, i, *tos):
            def step():
                for copy in copies(t, dz, i, 0, y_up):
                    copy.wait_recv()
                go(t, dz, i, *tos)

            steps.append(step)

        def across(place):
            dz = (0, -1, 1, -2, 2, -3, 3, 4)[place]
            came(1, dz, 1, *((y_up,) if place % 2 == 0 else ()))
            came(1, dz, 2, *((y_down,) if place % 2 == 1 else ()))

        def start():
            go(1, 0, 0, z_up, z_down)
            go(0, 0, 0, y_up, y_down, z_up, z_down)
            go(1, 0, 0, y_up, y_down)

        came(0, 0, 1, y_up, z_up, z_down)
        came(0, 0, 2, z_up, z_down)
        came(1, -1, 0, z_up, y_up, y_down)
        came(1, 1, 0, z_down, y_up, y_down)
        came(0, 0, 3, z_up, z_down)
        across(0)
        came(0, -1, 0, z_up)
        came(0, 1, 0, z_down)
        came(1, -2, 0, z_up, y_up, y_down)
        came(1, 2, 0, z_down, y_up, y_down)
        came(0, -1, 1, z_up)
        came(0, 1, 1, z_down)
        across(1)
        came(0, -1, 2, z_up)
        came(0, 1, 2, z_down)
        came(1, -3, 0, y_up, y_down)
        came(1, 3, 0, z_down, y_up, y_down)
        across(2)
        came(0, -1, 3, z_up)
        came(0, 1, 3, z_down)
        came(0, -2, 0, z_up)
        came(0, 2, 0, z_down)
        across(3)
        came(1, 4, 0, y_up, y_down)
        came(0, -2, 1, z_up)
        came(0, 2, 1, z_down)
        across(4)
        came(0, -2, 2, z_up)
        came(0, 2, 2, z_down)
        across(5)
        came(0, -2, 3, z_up)
        came(0, 2, 3, z_down)
        came(0, -3, 0, z_up)
        came(0, 3, 0)
        across(6)
        came(0, -3, 1)
        came(0, 3, 1, z_down)
        came(0, -3, 2, z_up)
        came(0, 3, 2)
        across(7)
        came(0, -3, 3)
        came(0, 3, 3, z_down)
        for i in range(4):
            came(0, 4, i)
        for dz in (0, -1, 1, -2, 2, -3, 3, 4):
            came(1, dz, 3)

        def finish():
            for copy in pending:
                copy.wait_send()

        return start, steps, finish

    def exchange(mine, theirs, ssem, rsem, slot):
        copy = remote(mine, theirs, ssem.at[slot], rsem.at[slot], other)
        copy.start()
        copy.wait()
        return mine[...] + theirs[...]

    llm_start, llm_steps, llm_finish = relay(
        (
            (lambda s: A.at[s, pl.ds(0, SPLIT)],),
            (lambda s: B.at[s], lambda s: A.at[s, pl.ds(SPLIT, 256 - SPLIT)]),
        ),
        send_llm, recv_llm,
    )
    for copy in own:
        copy.wait()

    own_rows = pl.ds(pl.multiple_of(c * 48, 16), 48)
    other_rows = pl.ds(pl.multiple_of(o * 48, 16), 48)
    image_other = remote(img2.at[o], henc.at[own_rows], misc_s.at[0], misc_r.at[0], other)

    @pl.when(x == 2)
    def _():
        spread = lax.broadcasted_iota(jnp.int32, (256, 128), 0)
        lane = lax.broadcasted_iota(jnp.int32, (256, 128), 1)
        for b in range(2 * BLOCKS):
            base = 100 * b // 128 * 128
            width = min(256, 3200 - base)
            pick = (spread == lane + (100 * b - base)) & (lane < 100)
            pick = jnp.where(pick, 1.0, 0.0).astype(BF16)[0:width]
            block = matmul(image[:, base : base + width], pick).astype(BF16)
            img2[b % 2, :, b // 2 * 128 : (b // 2 + 1) * 128] = block
        image_other.start()
        henc[own_rows, :] = img2[c]

    @pl.when(x == 2)
    def _():
        for source in (0, 1):
            for copy in gathered(source):
                copy.wait_recv()
        start, steps, finish = relay(
            ((lambda s: E1.at[s],), (lambda s: E2.at[s],)), send_enc, recv_enc
        )
        start()
        for step in steps:
            step()
        finish()

    @pl.when(x == 3)
    def _():
        for copy in gathered(2):
            copy.wait_recv()
        start, steps, finish = relay(
            (
                (lambda s: E1.at[s], lambda s: C1.at[s]),
                (lambda s: E2.at[s], lambda s: C2.at[s]),
            ),
            send_enc, recv_enc,
        )
        start()
        for step in steps:
            step()
        finish()

    llm_start()

    def text_local(j):
        return pltpu.make_async_copy(
            text.at[:, pl.ds(pl.multiple_of(j * 512 + c * 256, 256), 256)],
            h0.at[c, :, pl.ds(j * 256, 256)],
            text_l.at[j],
        )

    def text_other(j):
        return remote(
            text.at[:, pl.ds(pl.multiple_of(j * 512 + o * 256, 256), 256)],
            h0.at[c, :, pl.ds(j * 256, 256)],
            text_s.at[j], text_r.at[j], other,
        )

    def text_came(j):
        return remote(
            text.at[:, pl.ds(0, 256)],
            h0.at[o, :, pl.ds(j * 256, 256)],
            text_s.at[j], text_r.at[j], other,
        )

    marks_other = remote(ohb.at[c], ohb.at[c], misc_s.at[1], misc_r.at[1], other)

    @pl.when(x == 0)
    def _():
        spot = jnp.full((1, 128), -1.0, F32)
        for m in range(3):
            j = lax.broadcasted_iota(jnp.int32, (16, 128), 0)
            at = lax.broadcasted_iota(jnp.int32, (16, 128), 1)
            pick = jnp.where(at == j + (m * 16 + c * 48), 1.0, 0.0).astype(BF16)
            rows = (positions[m : m + 1, :] + (64 * m + 1)).astype(F32).astype(BF16)
            spot += matmul(jnp.broadcast_to(rows, (16, 16)), pick)[0:1]
        row = lax.broadcasted_iota(jnp.int32, (192, 128), 0).astype(F32)
        ohb[c] = jnp.where(row == spot, 1.0, 0.0).astype(BF16)
        marks_other.start()
        for j in range(BLOCKS):
            text_local(j).start()
            text_other(j).start()

    def projected(slot, weight):
        h = henc[...]
        es[slot, :, 0:128] = matmul(h, weight.reshape(BLOCKS * 128, 128))
        squares = jnp.zeros((96, 128), F32)
        for j in range(BLOCKS):
            part = h[:, j * 128 : (j + 1) * 128].astype(F32)
            squares += part * part
        es[slot, :, 128:256] = squares
        total = exchange(es.at[slot], er.at[slot], xe_s, xe_r, slot)
        scale = lax.rsqrt(
            jnp.sum(total[:, 128:256], axis=-1, keepdims=True) * (1.0 / 3200) + EPSILON
        )
        return gelu(total[:, 0:128] * scale).astype(BF16)

    passed = remote(henc, henc, misc_s.at[2], misc_r.at[2], x_next)
    pictures = remote(
        imgrows.at[pl.ds(0, 96)], imgrows.at[pl.ds(0, 96)], misc_s.at[3], misc_r.at[3], x_next
    )

    def encoder(plane):
        @pl.when(x == plane)
        def _():
            if plane == 2:
                image_other.wait_send()
                remote(
                    img2.at[c], henc.at[other_rows], misc_s.at[0], misc_r.at[0], other
                ).wait_recv()
            else:
                passed.wait_recv()

            def layer(l, _):
                k, half = l // 2, lax.rem(l, 2)
                activated = projected(half, E1[pl.ds(half * BLOCKS, BLOCKS), k])
                for j in range(BLOCKS):
                    branch = matmul(activated, E2[half * BLOCKS + j, k])
                    span = slice(j * 128, (j + 1) * 128)
                    henc[:, span] = (henc[:, span].astype(F32) + branch).astype(BF16)
                return 0

            lax.fori_loop(0, 4, layer, 0)
            if plane == 2:
                passed.start()
            else:
                latent = projected(0, C1[0:BLOCKS])[:, 0:64]
                for j in range(BLOCKS):
                    imgrows[0:96, j * 256 : (j + 1) * 256] = matmul(latent, C2[j]).astype(BF16)
                pictures.start()

    encoder(2)
    for number, step in enumerate(llm_steps):
        if number == TURN:
            encoder(3)
        step()
    llm_finish()

    @pl.when(x == 0)
    def _():
        marks_other.wait_send()
        remote(ohb.at[o], ohb.at[o], misc_s.at[1], misc_r.at[1], other).wait_recv()
        for j in range(BLOCKS):
            text_local(j).wait()
            text_other(j).wait_send()
            text_came(j).wait_recv()
        imgrows[96:128, :] = jnp.zeros((32, BLOCKS * 256), BF16)
        pictures.wait_recv()

    @pl.when(x == 3)
    def _():
        pictures.wait_send()

    @pl.when(x == 2)
    def _():
        passed.wait_send()

    for source in range(3):

        @pl.when(x == source)
        def _():
            for copy in gathered(source):
                copy.wait_send()

    def cols(j):
        return slice(j * 256, (j + 1) * 256)

    def folded(v):
        return v[:, 0:128] * v[:, 0:128] + v[:, 128:256] * v[:, 128:256]

    def activation(slot, acc, squares, meanwhile):
        xs[slot, :, 0:512] = acc
        xs[slot, :, 512:640] = squares
        copy = remote(xs.at[slot], xr.at[slot], x_s.at[slot], x_r.at[slot], other)
        copy.start()
        meanwhile()
        copy.wait()
        total = xs[slot] + xr[slot]
        scale = lax.rsqrt(
            jnp.sum(total[:, 512:640], axis=-1, keepdims=True) * (1.0 / 8192) + EPSILON
        )
        return silu(total[:, 0:512] * scale).astype(BF16)

    def span_of(start):
        return pl.ds(pl.multiple_of(start, 32), 32)

    def flow(k, start, part):
        span = hin.at[
            pl.ds(pl.multiple_of(2 * start, 64), 64), pl.ds(part * 1024, 1024)
        ]
        return remote(span, span, flow_s.at[k, part], flow_r.at[k, part], x_next)

    def result(k, start):
        rows = span_of(start)
        return remote(osend.at[rows], orecv.at[rows], out_s.at[k], out_r.at[k], other)

    def emit(k, start, source, base):
        mine = pl.ds(pl.multiple_of(base + c * 32, 32), 32)
        theirs = pl.ds(pl.multiple_of(base + o * 32, 32), 32)
        rows = span_of(start)
        osend[rows, :] = source[theirs, :]
        result(k, start).start()
        for j in range(BLOCKS):
            out[rows, pl.ds(pl.multiple_of(j * 512 + c * 256, 256), 256)] = source[mine, cols(j)]

    def merge(k, start):
        result(k, start).wait_recv()
        rows = span_of(start)
        for j in range(BLOCKS):
            out[rows, pl.ds(pl.multiple_of(j * 512 + o * 256, 256), 256)] = orecv[rows, cols(j)]

    crossing = remote(zout, zin, z_s.at[0], z_r.at[0], opposite)

    def chunk(k, start, halved, sent_last):
        base = pl.multiple_of(2 * start, 64)
        rows = span_of(start)
        both = pl.ds(base, 64)

        def give(layer):
            @pl.when(z_hi == layer)
            def _():
                emit(k, start, hin, base)

            if halved:

                @pl.when(z_hi != layer)
                def _():
                    zout[...] = hin[both, :]
                    crossing.start()

        @pl.when(x == 0)
        def _():
            marks = jnp.concatenate([ohb[0, rows, :], ohb[1, rows, :]], axis=0)
            hit = jnp.sum(marks.astype(F32), axis=-1, keepdims=True) > 0.5
            for j in range(BLOCKS):
                placed = matmul(marks, imgrows[:, cols(j)])
                words = jnp.concatenate([h0[0, rows, cols(j)], h0[1, rows, cols(j)]], axis=0)
                hin[both, cols(j)] = jnp.where(hit, placed, words.astype(F32)).astype(BF16)

        acc, squares = jnp.zeros((64, 512), F32), jnp.zeros((64, 128), F32)
        for part in range(4):

            @pl.when(x > 0)
            def _():
                flow(k, start, part).wait_recv()

            for j in range(4 * part, 4 * part + 4):
                h = hin[both, cols(j)]
                acc, squares = acc + matmul(h, A[j]), squares + folded(h.astype(F32))
        a = activation(0, acc, squares, lambda: None)
        acc, squares = jnp.zeros((64, 512), F32), jnp.zeros((64, 128), F32)
        for j in range(BLOCKS):
            h = (hin[both, cols(j)].astype(F32) + matmul(a, B[j])).astype(BF16)
            hin[both, cols(j)] = h
            acc, squares = acc + matmul(h, A[BLOCKS + j]), squares + folded(h.astype(F32))
        b = activation(1, acc, squares, lambda: give(0))
        for part in range(4):
            for j in range(4 * part, 4 * part + 4):
                h = hin[both, cols(j)].astype(F32) + matmul(b, B[BLOCKS + j])
                hin[both, cols(j)] = h.astype(BF16)

            @pl.when(x < 3)
            def _():
                sent_last(part)
                flow(k, start, part).start()

        give(1)

    first = z_hi * 32
    chunk(0, first, True, lambda part: None)

    def shared(k, _):
        def sent_last(part):
            @pl.when(k == 1)
            def _():
                flow(0, first, part).wait_send()

            @pl.when(k > 1)
            def _():
                flow(k - 1, 32 * k, part).wait_send()

        chunk(k, 32 * k + 32, False, sent_last)

        @pl.when(k == 1)
        def _():
            merge(0, first)

        @pl.when(k > 1)
        def _():
            merge(k - 1, 32 * k)

        return 0

    lax.fori_loop(1, 5, shared, 0)
    crossing.wait_recv()
    emit(5, 32 - first, zin, 0)
    merge(4, 160)
    merge(5, 32 - first)
    crossing.wait_send()
    result(0, first).wait_send()
    result(5, 32 - first).wait_send()

    def drain(k, _):
        result(k, 32 * k + 32).wait_send()
        return 0

    lax.fori_loop(1, 5, drain, 0)

    @pl.when(x < 3)
    def _():
        for part in range(4):
            flow(4, 160, part).wait_send()


def local(text, image, positions, enc_in, enc_out, conn_in, conn_out, llm_in, llm_out):
    any_spec = pl.BlockSpec(memory_space=pl.ANY)
    vmem_spec = pl.BlockSpec(memory_space=pltpu.VMEM)
    dma = pltpu.SemaphoreType.DMA
    hidden = pl.pallas_call(
        kernel,
        out_shape=jax.ShapeDtypeStruct((192, 8192), BF16),
        in_specs=[any_spec] + [vmem_spec] * 6 + [any_spec] * 2,
        out_specs=vmem_spec,
        scratch_shapes=[
            pltpu.VMEM((32, 256, 512), BF16),
            pltpu.VMEM((32, 512, 256), BF16),
            pltpu.VMEM((32, 2, 128, 128), BF16),
            pltpu.VMEM((32, 2, 128, 128), BF16),
            pltpu.VMEM((32, 128, 128), BF16),
            pltpu.VMEM((32, 64, 256), BF16),
            pltpu.VMEM((2, 128, 128), BF16),
            pltpu.VMEM((2, 192, 4096), BF16),
            pltpu.VMEM((2, 192, 128), BF16),
            pltpu.VMEM((2, 48, 2048), BF16),
            pltpu.VMEM((96, 2048), BF16),
            pltpu.VMEM((128, 4096), BF16),
            pltpu.VMEM((2, 64, 640), F32),
            pltpu.VMEM((2, 64, 640), F32),
            pltpu.VMEM((2, 96, 256), F32),
            pltpu.VMEM((2, 96, 256), F32),
            pltpu.VMEM((384, 4096), BF16),
            pltpu.VMEM((192, 4096), BF16),
            pltpu.VMEM((192, 4096), BF16),
            pltpu.VMEM((64, 4096), BF16),
            pltpu.VMEM((64, 4096), BF16),
            dma((3, 31)),
            dma((3, 32)),
            dma((4, 31)),
            dma((4, 32)),
            dma((2,)),
            dma((2, 2)),
            dma((2,)),
            dma((16,)),
            dma((16,)),
            dma((16,)),
            dma((4,)),
            dma((4,)),
            dma((2,)),
            dma((2,)),
            dma((2,)),
            dma((2,)),
            dma((5, 4)),
            dma((5, 4)),
            dma((6,)),
            dma((6,)),
            dma((1,)),
            dma((1,)),
        ],
        compiler_params=pltpu.CompilerParams(
            collective_id=0, has_side_effects=True, vmem_limit_bytes=60 * 1024 * 1024
        ),
        cost_estimate=pl.CostEstimate(
            flops=14_000_000_000, bytes_accessed=16_000_000, transcendentals=1_000_000
        ),
    )(text, image, positions, enc_in[0], enc_out[0], conn_in, conn_out, llm_in[0], llm_out[0])
    return hidden[None]


def solution(mesh):
    return jax.shard_map(
        local,
        mesh=mesh,
        in_specs=(
            P("dp", None),
            P("dp", None),
            P("dp", None),
            P("section", "dp", None),
            P("section", None, "dp"),
            P("dp", None),
            P(None, "dp"),
            P("section", "dp", None),
            P("section", None, "dp"),
        ),
        out_specs=P("section", "dp", None),
        check_vma=False,
    )
```

```python
import jax
import jax.numpy as jnp
from jax import lax
from jax.experimental import pallas as pl
from jax.experimental.pallas import tpu as pltpu
from jax.sharding import PartitionSpec as P

EPSILON = 1e-06
MESH = pl.DeviceIdType.MESH
F32 = jnp.float32
BF16 = jnp.bfloat16
SPLIT = 208
TURN = 3
BLOCKS = 16


def gelu(v):
    return 0.5 * v * (1.0 + lax.erf(v * 0.7071067811865476))


def matmul_t(a, b):
    return lax.dot_general(a, b, (((1,), (1,)), ((), ())), preferred_element_type=F32)


def silu(v):
    return v / (1.0 + jnp.exp(-v))


def matmul(a, b):
    return jnp.dot(a, b, preferred_element_type=F32)


def device(x, y, z, c):
    return (x * 2 + z // 4, lax.rem(z, 4) * 8 + y * 2 + c)


def kernel(
    text, image, positions, enc_in, enc_out, conn_in, conn_out, wa, wb, out,
    A, B, E1, E2, C1, C2, ep, h0, ohb, img2, henc, imgrows, xs, xr, es, er, hin, osend, orecv,
    zout, zin, zby,
    send_llm, recv_llm, send_enc, recv_enc, gather_s, gather_r, own_sem, text_l, text_s, text_r,
    misc_s, misc_r, x_s, x_r, xe_s, xe_r, flow_s, flow_r, out_s, out_r, z_s, z_r, by_s, by_r,
):
    section = lax.axis_index("section")
    dp = lax.axis_index("dp")
    x, z_hi = section // 2, lax.rem(section, 2)
    z = z_hi * 4 + dp // 8
    y = lax.rem(dp // 2, 4)
    c = lax.rem(dp, 2)
    o = 1 - c
    me = z * 4 + y

    def up(v, by, n):
        return lax.rem(v + by + n, n)

    y_up, y_down = device(x, up(y, 1, 4), z, c), device(x, up(y, -1, 4), z, c)
    z_up, z_down = device(x, y, up(z, 1, 8), c), device(x, y, up(z, -1, 8), c)
    other = device(x, y, z, o)
    x_next = device(up(x, 1, 4), y, z, c)
    x_last = device(up(x, -1, 4), y, z, c)
    x_far = device(up(x, 2, 4), y, z, c)
    opposite = device(x, y, up(z, 4, 8), c)

    def remote(src, dst, ssem, rsem, to):
        return pltpu.make_async_remote_copy(
            src_ref=src, dst_ref=dst, send_sem=ssem, recv_sem=rsem, device_id=to, device_id_type=MESH
        )

    barrier = pltpu.get_barrier_semaphore()
    for to in (y_up, y_down, z_up, z_down, other, x_next, x_last, x_far, opposite):
        pl.semaphore_signal(barrier, inc=1, device_id=to, device_id_type=MESH)

    own = [
        pltpu.make_async_copy(wa, A.at[me], own_sem.at[0]),
        pltpu.make_async_copy(wb, B.at[me], own_sem.at[1]),
    ]
    for copy in own:
        copy.start()
    blank = jnp.zeros((128, 128), BF16)
    ep[0] = blank
    ep[1] = blank
    ep[0, 0:100, :] = enc_in[...]
    ep[1, 0:100, :] = enc_out[...]

    @pl.when(x == 3)
    def _():
        C1[me] = blank
        C1[me, 0:64, 0:100] = conn_in[...]
        C2[me] = conn_out[...]
        E1[me, 1] = ep[0]
        E2[me, 1] = ep[1]

    pl.semaphore_wait(barrier, 9)

    def gathered(source):
        to = device(max(2, source + 1), y, z, c)
        k = source % 2
        return [
            remote(ep.at[e], place.at[me, k], gather_s.at[e], gather_r.at[e, k], to)
            for e, place in ((0, E1), (1, E2))
        ]

    for source in range(3):

        @pl.when(x == source)
        def _():
            for copy in gathered(source):
                copy.start()

    def relay(groups, send, recv):
        first_of = (0, len(groups[0]))
        sent = [0, 0]
        pending = []
        steps = []
        y_at = (y, up(y, -1, 4), up(y, 1, 4), up(y, 2, 4))

        def copies(t, dz, i, number, to):
            slot = up(z, dz, 8) * 4 + y_at[i]
            return [
                remote(
                    part(slot), part(slot),
                    send.at[first_of[t] + e, number], recv.at[first_of[t] + e, slot], to,
                )
                for e, part in enumerate(groups[t])
            ]

        def go(t, dz, i, *tos):
            for to in tos:
                for copy in copies(t, dz, i, sent[t], to):
                    copy.start()
                    pending.append(copy)
                sent[t] += 1

        def came(t, dz, i, *tos):
            def step():
                for copy in copies(t, dz, i, 0, y_up):
                    copy.wait_recv()
                go(t, dz, i, *tos)

            steps.append(step)

        def across(place):
            dz = (0, -1, 1, -2, 2, -3, 3, 4)[place]
            came(1, dz, 1, *((y_up,) if place % 2 == 0 else ()))
            came(1, dz, 2, *((y_down,) if place % 2 == 1 else ()))

        def start():
            go(1, 0, 0, z_up, z_down)
            go(0, 0, 0, y_up, y_down, z_up, z_down)
            go(1, 0, 0, y_up, y_down)

        came(0, 0, 1, y_up, z_up, z_down)
        came(0, 0, 2, z_up, z_down)
        came(1, -1, 0, z_up, y_up, y_down)
        came(1, 1, 0, z_down, y_up, y_down)
        came(0, 0, 3, z_up, z_down)
        across(0)
        came(0, -1, 0, z_up)
        came(0, 1, 0, z_down)
        came(1, -2, 0, z_up, y_up, y_down)
        came(1, 2, 0, z_down, y_up, y_down)
        came(0, -1, 1, z_up)
        came(0, 1, 1, z_down)
        across(1)
        came(0, -1, 2, z_up)
        came(0, 1, 2, z_down)
        came(1, -3, 0, y_up, y_down)
        came(1, 3, 0, z_down, y_up, y_down)
        across(2)
        came(0, -1, 3, z_up)
        came(0, 1, 3, z_down)
        came(0, -2, 0, z_up)
        came(0, 2, 0, z_down)
        across(3)
        came(1, 4, 0, y_up, y_down)
        came(0, -2, 1, z_up)
        came(0, 2, 1, z_down)
        across(4)
        came(0, -2, 2, z_up)
        came(0, 2, 2, z_down)
        across(5)
        came(0, -2, 3, z_up)
        came(0, 2, 3, z_down)
        came(0, -3, 0, z_up)
        came(0, 3, 0)
        across(6)
        came(0, -3, 1)
        came(0, 3, 1, z_down)
        came(0, -3, 2, z_up)
        came(0, 3, 2)
        across(7)
        came(0, -3, 3)
        came(0, 3, 3, z_down)
        for i in range(4):
            came(0, 4, i)
        for dz in (0, -1, 1, -2, 2, -3, 3, 4):
            came(1, dz, 3)

        def finish():
            for copy in pending:
                copy.wait_send()

        return start, steps, finish

    def exchange(mine, theirs, ssem, rsem, slot):
        copy = remote(mine, theirs, ssem.at[slot], rsem.at[slot], other)
        copy.start()
        copy.wait()
        return mine[...] + theirs[...]

    llm_start, llm_steps, llm_finish = relay(
        (
            (lambda s: A.at[s, pl.ds(0, SPLIT)],),
            (lambda s: B.at[s], lambda s: A.at[s, pl.ds(SPLIT, 256 - SPLIT)]),
        ),
        send_llm, recv_llm,
    )
    for copy in own:
        copy.wait()

    own_rows = pl.ds(pl.multiple_of(c * 48, 16), 48)
    other_rows = pl.ds(pl.multiple_of(o * 48, 16), 48)
    image_other = remote(img2.at[o], henc.at[own_rows], misc_s.at[0], misc_r.at[0], other)

    @pl.when(x == 2)
    def _():
        spread = lax.broadcasted_iota(jnp.int32, (256, 128), 0)
        lane = lax.broadcasted_iota(jnp.int32, (256, 128), 1)
        for b in range(2 * BLOCKS):
            base = 100 * b // 128 * 128
            width = min(256, 3200 - base)
            pick = (spread == lane + (100 * b - base)) & (lane < 100)
            pick = jnp.where(pick, 1.0, 0.0).astype(BF16)[0:width]
            block = matmul(image[:, base : base + width], pick).astype(BF16)
            img2[b % 2, :, b // 2 * 128 : (b // 2 + 1) * 128] = block
        image_other.start()
        henc[own_rows, :] = img2[c]

    @pl.when(x == 2)
    def _():
        for source in (0, 1):
            for copy in gathered(source):
                copy.wait_recv()
        start, steps, finish = relay(
            ((lambda s: E1.at[s],), (lambda s: E2.at[s],)), send_enc, recv_enc
        )
        start()
        for step in steps:
            step()
        finish()

    @pl.when(x == 3)
    def _():
        for copy in gathered(2):
            copy.wait_recv()
        start, steps, finish = relay(
            (
                (lambda s: E1.at[s], lambda s: C1.at[s]),
                (lambda s: E2.at[s], lambda s: C2.at[s]),
            ),
            send_enc, recv_enc,
        )
        start()
        for step in steps:
            step()
        finish()

    llm_start()

    def text_local(j):
        return pltpu.make_async_copy(
            text.at[:, pl.ds(pl.multiple_of(j * 512 + c * 256, 256), 256)],
            h0.at[c, :, pl.ds(j * 256, 256)],
            text_l.at[j],
        )

    def text_other(j):
        return remote(
            text.at[:, pl.ds(pl.multiple_of(j * 512 + o * 256, 256), 256)],
            h0.at[c, :, pl.ds(j * 256, 256)],
            text_s.at[j], text_r.at[j], other,
        )

    def text_came(j):
        return remote(
            text.at[:, pl.ds(0, 256)],
            h0.at[o, :, pl.ds(j * 256, 256)],
            text_s.at[j], text_r.at[j], other,
        )

    marks_other = remote(ohb.at[c], ohb.at[c], misc_s.at[1], misc_r.at[1], other)

    @pl.when(x == 0)
    def _():
        spot = jnp.full((1, 128), -1.0, F32)
        for m in range(3):
            j = lax.broadcasted_iota(jnp.int32, (16, 128), 0)
            at = lax.broadcasted_iota(jnp.int32, (16, 128), 1)
            pick = jnp.where(at == j + (m * 16 + c * 48), 1.0, 0.0).astype(BF16)
            rows = (positions[m : m + 1, :] + (64 * m + 1)).astype(F32).astype(BF16)
            spot += matmul(jnp.broadcast_to(rows, (16, 16)), pick)[0:1]
        row = lax.broadcasted_iota(jnp.int32, (192, 128), 0).astype(F32)
        ohb[c] = jnp.where(row == spot, 1.0, 0.0).astype(BF16)
        marks_other.start()
        for j in range(BLOCKS):
            text_local(j).start()
            text_other(j).start()

    def projected(slot, product):
        h = henc[...]
        es[slot, :, 0:128] = product(h)
        squares = jnp.zeros((96, 128), F32)
        for j in range(BLOCKS):
            part = h[:, j * 128 : (j + 1) * 128].astype(F32)
            squares += part * part
        es[slot, :, 128:256] = squares
        total = exchange(es.at[slot], er.at[slot], xe_s, xe_r, slot)
        scale = lax.rsqrt(
            jnp.sum(total[:, 128:256], axis=-1, keepdims=True) * (1.0 / 3200) + EPSILON
        )
        return gelu(total[:, 0:128] * scale).astype(BF16)

    passed = remote(henc, henc, misc_s.at[2], misc_r.at[2], x_next)
    pictures = remote(
        imgrows.at[pl.ds(0, 96)], imgrows.at[pl.ds(0, 96)], misc_s.at[3], misc_r.at[3], x_next
    )

    def encoder(plane):
        @pl.when(x == plane)
        def _():
            if plane == 2:
                image_other.wait_send()
                remote(
                    img2.at[c], henc.at[other_rows], misc_s.at[0], misc_r.at[0], other
                ).wait_recv()
            else:
                passed.wait_recv()

            def layer(l, _):
                k, half = l // 2, lax.rem(l, 2)
                weight = E1[pl.ds(half * BLOCKS, BLOCKS), k].reshape(BLOCKS * 128, 128)
                activated = projected(half, lambda h: matmul(h, weight))
                for j in range(BLOCKS):
                    branch = matmul_t(activated, E2[half * BLOCKS + j, k])
                    span = slice(j * 128, (j + 1) * 128)
                    henc[:, span] = (henc[:, span].astype(F32) + branch).astype(BF16)
                return 0

            lax.fori_loop(0, 4, layer, 0)
            if plane == 2:
                passed.start()
            else:

                def to_latent(h):
                    total = jnp.zeros((96, 128), F32)
                    for j in range(BLOCKS):
                        total += matmul_t(h[:, j * 128 : (j + 1) * 128], C1[j])
                    return total

                latent = projected(0, to_latent)[:, 0:64]
                for j in range(BLOCKS):
                    imgrows[0:96, j * 256 : (j + 1) * 256] = matmul(latent, C2[j]).astype(BF16)
                pictures.start()

    def cols(j):
        return slice(j * 256, (j + 1) * 256)

    def first_state():
        @pl.when(x == 0)
        def _():
            marks_other.wait_send()
            remote(ohb.at[o], ohb.at[o], misc_s.at[1], misc_r.at[1], other).wait_recv()
            for j in range(BLOCKS):
                text_local(j).wait()
                text_other(j).wait_send()
                text_came(j).wait_recv()
            imgrows[96:128, :] = jnp.zeros((32, BLOCKS * 256), BF16)
            pictures.wait_recv()

            def place(k, _):
                rows = pl.ds(pl.multiple_of(32 * k, 32), 32)
                both = pl.ds(pl.multiple_of(64 * k, 64), 64)
                marks = jnp.concatenate([ohb[0, rows, :], ohb[1, rows, :]], axis=0)
                hit = jnp.sum(marks.astype(F32), axis=-1, keepdims=True) > 0.5
                for j in range(BLOCKS):
                    placed = matmul(marks, imgrows[:, cols(j)])
                    words = jnp.concatenate([h0[0, rows, cols(j)], h0[1, rows, cols(j)]], axis=0)
                    hin[both, cols(j)] = jnp.where(hit, placed, words.astype(F32)).astype(BF16)
                return 0

            lax.fori_loop(0, 6, place, 0)

    encoder(2)
    for number, step in enumerate(llm_steps):
        if number == TURN:
            encoder(3)
        if number == len(llm_steps) - 12:
            first_state()
        step()
    llm_finish()

    @pl.when(x == 3)
    def _():
        pictures.wait_send()

    @pl.when(x == 2)
    def _():
        passed.wait_send()

    for source in range(3):

        @pl.when(x == source)
        def _():
            for copy in gathered(source):
                copy.wait_send()

    def folded(v):
        return v[:, 0:128] * v[:, 0:128] + v[:, 128:256] * v[:, 128:256]

    def activation(slot, acc, squares, meanwhile):
        xs[slot, :, 0:512] = acc
        xs[slot, :, 512:640] = squares
        copy = remote(xs.at[slot], xr.at[slot], x_s.at[slot], x_r.at[slot], other)
        copy.start()
        meanwhile()
        copy.wait()
        total = xs[slot] + xr[slot]
        scale = lax.rsqrt(
            jnp.sum(total[:, 512:640], axis=-1, keepdims=True) * (1.0 / 8192) + EPSILON
        )
        return silu(total[:, 0:512] * scale).astype(BF16)

    def span_of(start):
        return pl.ds(pl.multiple_of(start, 32), 32)

    def flow(k, start, part):
        span = hin.at[
            pl.ds(pl.multiple_of(2 * start, 64), 64), pl.ds(part * 1024, 1024)
        ]
        return remote(span, span, flow_s.at[k, part], flow_r.at[k, part], x_next)

    def result(k, start):
        rows = span_of(start)
        return remote(osend.at[rows], orecv.at[rows], out_s.at[k], out_r.at[k], other)

    def emit(k, start, source, base):
        mine = pl.ds(pl.multiple_of(base + c * 32, 32), 32)
        theirs = pl.ds(pl.multiple_of(base + o * 32, 32), 32)
        rows = span_of(start)
        osend[rows, :] = source[theirs, :]
        result(k, start).start()
        for j in range(BLOCKS):
            out[rows, pl.ds(pl.multiple_of(j * 512 + c * 256, 256), 256)] = source[mine, cols(j)]

    def merge(k, start):
        result(k, start).wait_recv()
        rows = span_of(start)
        for j in range(BLOCKS):
            out[rows, pl.ds(pl.multiple_of(j * 512 + o * 256, 256), 256)] = orecv[rows, cols(j)]

    def crossing(n):
        k = min(n, 1)
        span = pl.ds((0, 0, 2048)[n], (4096, 2048, 2048)[n])
        return remote(zout.at[k, :, span], zin.at[k, :, span], z_s.at[n], z_r.at[n], opposite)

    def leg(n, part):
        near = pl.ds(part * 1024, 1024)
        far = pl.ds(2048 + part * 1024, 1024)
        src = (zout.at[1, :, far], zby.at[0, :, near], zby.at[1, :, near])[n]
        dst = (zby.at[0, :, near], zby.at[1, :, near], zin.at[1, :, far])[n]
        to = (x_next, opposite, x_last)[n]
        return remote(src, dst, by_s.at[n, part], by_r.at[n, part], to)

    def cross(k):
        if k == 0:
            crossing(0).start()
            return
        crossing(1).start()

        @pl.when(x < 3)
        def _():
            crossing(2).start()

        @pl.when(x == 3)
        def _():
            for part in range(2):
                leg(0, part).start()

    def chunk(k, start, halved, sent_last):
        base = pl.multiple_of(2 * start, 64)
        rows = span_of(start)
        both = pl.ds(base, 64)

        def give(layer):
            @pl.when(z_hi == layer)
            def _():
                emit(k, start, hin, base)

            if halved:

                @pl.when(z_hi != layer)
                def _():
                    zout[k] = hin[both, :]
                    cross(k)

        acc, squares = jnp.zeros((64, 512), F32), jnp.zeros((64, 128), F32)
        for part in range(4):

            @pl.when(x > 0)
            def _():
                flow(k, start, part).wait_recv()

            for j in range(4 * part, 4 * part + 4):
                h = hin[both, cols(j)]
                acc, squares = acc + matmul(h, A[j]), squares + folded(h.astype(F32))
        a = activation(0, acc, squares, lambda: None)
        acc, squares = jnp.zeros((64, 512), F32), jnp.zeros((64, 128), F32)
        for j in range(BLOCKS):
            h = (hin[both, cols(j)].astype(F32) + matmul(a, B[j])).astype(BF16)
            hin[both, cols(j)] = h
            acc, squares = acc + matmul(h, A[BLOCKS + j]), squares + folded(h.astype(F32))
        b = activation(1, acc, squares, lambda: give(0))
        for part in range(4):
            for j in range(4 * part, 4 * part + 4):
                h = hin[both, cols(j)].astype(F32) + matmul(b, B[BLOCKS + j])
                hin[both, cols(j)] = h.astype(BF16)

            @pl.when(x < 3)
            def _():
                sent_last(part)
                flow(k, start, part).start()

        give(1)

    first = z_hi * 64
    across_first = 64 - first
    chunk(0, first, True, lambda part: None)
    chunk(1, first + 32, True, lambda part: flow(0, first, part).wait_send())
    merge(0, first)

    def shared(k, _):
        def sent_last(part):
            @pl.when(k == 2)
            def _():
                flow(1, first + 32, part).wait_send()

            @pl.when(k > 2)
            def _():
                flow(k - 1, 32 * k + 32, part).wait_send()

        chunk(k, 32 * k + 64, False, sent_last)

        @pl.when(k == 2)
        def _():
            merge(1, first + 32)

        @pl.when(k > 2)
        def _():
            merge(k - 1, 32 * k + 32)

        return 0

    lax.fori_loop(2, 4, shared, 0)
    crossing(0).wait_recv()
    emit(4, across_first, zin.at[0], 0)
    merge(3, 160)
    crossing(1).wait_recv()

    @pl.when(x < 3)
    def _():
        crossing(2).wait_recv()

    @pl.when(x == 3)
    def _():
        for part in range(2):
            leg(2, part).wait_recv()

    emit(5, across_first + 32, zin.at[1], 0)
    for k in range(2):
        merge(4 + k, across_first + 32 * k)
        result(k, first + 32 * k).wait_send()
        result(2 + k, 128 + 32 * k).wait_send()
        result(4 + k, across_first + 32 * k).wait_send()
        crossing(k).wait_send()

    @pl.when(x < 3)
    def _():
        crossing(2).wait_send()

    @pl.when(x == 3)
    def _():
        for part in range(2):
            leg(0, part).wait_send()

    @pl.when(x == 0)
    def _():
        for n in (0, 1):
            for part in range(2):
                leg(n, part).wait_recv()
                leg(n + 1, part).start()
        for n in (1, 2):
            for part in range(2):
                leg(n, part).wait_send()

    @pl.when(x < 3)
    def _():
        for part in range(4):
            flow(3, 160, part).wait_send()


def local(text, image, positions, enc_in, enc_out, conn_in, conn_out, llm_in, llm_out):
    hbm_spec = pl.BlockSpec(memory_space=pltpu.HBM)
    vmem_spec = pl.BlockSpec(memory_space=pltpu.VMEM)
    dma = pltpu.SemaphoreType.DMA
    hidden = pl.pallas_call(
        kernel,
        out_shape=jax.ShapeDtypeStruct((192, 8192), BF16),
        in_specs=[hbm_spec] + [vmem_spec] * 6 + [hbm_spec] * 2,
        out_specs=vmem_spec,
        scratch_shapes=[
            pltpu.VMEM((32, 256, 512), BF16),
            pltpu.VMEM((32, 512, 256), BF16),
            pltpu.VMEM((32, 2, 128, 128), BF16),
            pltpu.VMEM((32, 2, 128, 128), BF16),
            pltpu.VMEM((32, 128, 128), BF16),
            pltpu.VMEM((32, 64, 256), BF16),
            pltpu.VMEM((2, 128, 128), BF16),
            pltpu.VMEM((2, 192, 4096), BF16),
            pltpu.VMEM((2, 192, 128), BF16),
            pltpu.VMEM((2, 48, 2048), BF16),
            pltpu.VMEM((96, 2048), BF16),
            pltpu.VMEM((128, 4096), BF16),
            pltpu.VMEM((2, 64, 640), F32),
            pltpu.VMEM((2, 64, 640), F32),
            pltpu.VMEM((2, 96, 256), F32),
            pltpu.VMEM((2, 96, 256), F32),
            pltpu.VMEM((384, 4096), BF16),
            pltpu.VMEM((192, 4096), BF16),
            pltpu.VMEM((192, 4096), BF16),
            pltpu.VMEM((2, 64, 4096), BF16),
            pltpu.VMEM((2, 64, 4096), BF16),
            pltpu.VMEM((2, 64, 2048), BF16),
            dma((3, 31)),
            dma((3, 32)),
            dma((4, 31)),
            dma((4, 32)),
            dma((2,)),
            dma((2, 2)),
            dma((2,)),
            dma((16,)),
            dma((16,)),
            dma((16,)),
            dma((4,)),
            dma((4,)),
            dma((2,)),
            dma((2,)),
            dma((2,)),
            dma((2,)),
            dma((4, 4)),
            dma((4, 4)),
            dma((6,)),
            dma((6,)),
            dma((3,)),
            dma((3,)),
            dma((3, 2)),
            dma((3, 2)),
        ],
        compiler_params=pltpu.CompilerParams(
            collective_id=0, has_side_effects=True, vmem_limit_bytes=50 * 1024 * 1024
        ),
        cost_estimate=pl.CostEstimate(
            flops=14_000_000_000, bytes_accessed=16_000_000, transcendentals=1_000_000
        ),
    )(
        text, image, positions, enc_in[0], enc_out[0].T, conn_in.T, conn_out, llm_in[0], llm_out[0]
    )
    return hidden[None]


def solution(mesh):
    return jax.shard_map(
        local,
        mesh=mesh,
        in_specs=(
            P("dp", None),
            P("dp", None),
            P("dp", None),
            P("section", "dp", None),
            P("section", None, "dp"),
            P("dp", None),
            P(None, "dp"),
            P("section", "dp", None),
            P("section", None, "dp"),
        ),
        out_specs=P("section", "dp", None),
        check_vma=False,
    )
```

```python
import jax
import jax.numpy as jnp
from jax import lax
from jax.experimental import pallas as pl
from jax.experimental.pallas import tpu as pltpu
from jax.sharding import PartitionSpec as P

EPSILON = 1e-06
MESH = pl.DeviceIdType.MESH
F32 = jnp.float32
BF16 = jnp.bfloat16
SPLIT = 208
TURN = 3
BLOCKS = 16


def gelu(v):
    return 0.5 * v * (1.0 + lax.erf(v * 0.7071067811865476))


def matmul_t(a, b):
    return lax.dot_general(a, b, (((1,), (1,)), ((), ())), preferred_element_type=F32)


def silu(v):
    return v / (1.0 + jnp.exp(-v))


def matmul(a, b):
    return jnp.dot(a, b, preferred_element_type=F32)


def device(x, y, z, c):
    return (x * 2 + z // 4, lax.rem(z, 4) * 8 + y * 2 + c)


def kernel(
    text, image, positions, enc_in, enc_out, conn_in, conn_out, wa, wb, out,
    A, B, E1, E2, C1, C2, ep, h0, ohb, img2, henc, imgrows, xs, xr, es, er, hin, osend, orecv,
    zout, zin, zby,
    send_llm, recv_llm, send_enc, recv_enc, gather_s, gather_r, own_sem, text_l, text_s, text_r,
    misc_s, misc_r, x_s, x_r, xe_s, xe_r, flow_s, flow_r, out_s, out_r, z_s, z_r, by_s, by_r,
):
    section = lax.axis_index("section")
    dp = lax.axis_index("dp")
    x, z_hi = section // 2, lax.rem(section, 2)
    z = z_hi * 4 + dp // 8
    y = lax.rem(dp // 2, 4)
    c = lax.rem(dp, 2)
    o = 1 - c
    me = z * 4 + y

    def up(v, by, n):
        return lax.rem(v + by + n, n)

    y_up, y_down = device(x, up(y, 1, 4), z, c), device(x, up(y, -1, 4), z, c)
    z_up, z_down = device(x, y, up(z, 1, 8), c), device(x, y, up(z, -1, 8), c)
    other = device(x, y, z, o)
    x_next = device(up(x, 1, 4), y, z, c)
    x_last = device(up(x, -1, 4), y, z, c)
    x_far = device(up(x, 2, 4), y, z, c)
    opposite = device(x, y, up(z, 4, 8), c)

    def remote(src, dst, ssem, rsem, to):
        return pltpu.make_async_remote_copy(
            src_ref=src, dst_ref=dst, send_sem=ssem, recv_sem=rsem, device_id=to, device_id_type=MESH
        )

    barrier = pltpu.get_barrier_semaphore()
    for to in (y_up, y_down, z_up, z_down, other, x_next, x_last, x_far, opposite):
        pl.semaphore_signal(barrier, inc=1, device_id=to, device_id_type=MESH)

    own = [
        pltpu.make_async_copy(wa, A.at[me], own_sem.at[0]),
        pltpu.make_async_copy(wb, B.at[me], own_sem.at[1]),
    ]
    for copy in own:
        copy.start()
    blank = jnp.zeros((128, 128), BF16)
    ep[0] = blank
    ep[1] = blank
    ep[0, 0:100, :] = enc_in[...]
    ep[1, 0:100, :] = enc_out[...]

    @pl.when(x == 3)
    def _():
        C1[me] = blank
        C1[me, 0:64, 0:100] = conn_in[...]
        C2[me] = conn_out[...]
        E1[me, 1] = ep[0]
        E2[me, 1] = ep[1]

    pl.semaphore_wait(barrier, 9)

    def gathered(source):
        to = device(max(2, source + 1), y, z, c)
        k = source % 2
        return [
            remote(ep.at[e], place.at[me, k], gather_s.at[e], gather_r.at[e, k], to)
            for e, place in ((0, E1), (1, E2))
        ]

    for source in range(3):

        @pl.when(x == source)
        def _():
            for copy in gathered(source):
                copy.start()

    def relay(groups, send, recv):
        first_of = (0, len(groups[0]))
        sent = [0, 0]
        pending = []
        steps = []
        y_at = (y, up(y, -1, 4), up(y, 1, 4), up(y, 2, 4))

        def copies(t, dz, i, number, to):
            slot = up(z, dz, 8) * 4 + y_at[i]
            return [
                remote(
                    part(slot), part(slot),
                    send.at[first_of[t] + e, number], recv.at[first_of[t] + e, slot], to,
                )
                for e, part in enumerate(groups[t])
            ]

        def go(t, dz, i, *tos):
            for to in tos:
                for copy in copies(t, dz, i, sent[t], to):
                    copy.start()
                    pending.append(copy)
                sent[t] += 1

        def came(t, dz, i, *tos):
            def step():
                for copy in copies(t, dz, i, 0, y_up):
                    copy.wait_recv()
                go(t, dz, i, *tos)

            steps.append(step)

        def across(place):
            dz = (0, -1, 1, -2, 2, -3, 3, 4)[place]
            came(1, dz, 1, *((y_up,) if place % 2 == 0 else ()))
            came(1, dz, 2, *((y_down,) if place % 2 == 1 else ()))

        def start():
            go(1, 0, 0, z_up, z_down)
            go(0, 0, 0, y_up, y_down, z_up, z_down)
            go(1, 0, 0, y_up, y_down)

        came(0, 0, 1, y_up, z_up, z_down)
        came(0, 0, 2, z_up, z_down)
        came(1, -1, 0, z_up, y_up, y_down)
        came(1, 1, 0, z_down, y_up, y_down)
        came(0, 0, 3, z_up, z_down)
        across(0)
        came(0, -1, 0, z_up)
        came(0, 1, 0, z_down)
        came(1, -2, 0, z_up, y_up, y_down)
        came(1, 2, 0, z_down, y_up, y_down)
        came(0, -1, 1, z_up)
        came(0, 1, 1, z_down)
        across(1)
        came(0, -1, 2, z_up)
        came(0, 1, 2, z_down)
        came(1, -3, 0, y_up, y_down)
        came(1, 3, 0, z_down, y_up, y_down)
        across(2)
        came(0, -1, 3, z_up)
        came(0, 1, 3, z_down)
        came(0, -2, 0, z_up)
        came(0, 2, 0, z_down)
        across(3)
        came(1, 4, 0, y_up, y_down)
        came(0, -2, 1, z_up)
        came(0, 2, 1, z_down)
        across(4)
        came(0, -2, 2, z_up)
        came(0, 2, 2, z_down)
        across(5)
        came(0, -2, 3, z_up)
        came(0, 2, 3, z_down)
        came(0, -3, 0, z_up)
        came(0, 3, 0)
        across(6)
        came(0, -3, 1)
        came(0, 3, 1, z_down)
        came(0, -3, 2, z_up)
        came(0, 3, 2)
        across(7)
        came(0, -3, 3)
        came(0, 3, 3, z_down)
        for i in range(4):
            came(0, 4, i)
        for dz in (0, -1, 1, -2, 2, -3, 3, 4):
            came(1, dz, 3)

        def finish():
            for copy in pending:
                copy.wait_send()

        return start, steps, finish

    def exchange(mine, theirs, ssem, rsem, slot):
        copy = remote(mine, theirs, ssem.at[slot], rsem.at[slot], other)
        copy.start()
        copy.wait()
        return mine[...] + theirs[...]

    llm_start, llm_steps, llm_finish = relay(
        (
            (lambda s: A.at[s, pl.ds(0, SPLIT)],),
            (lambda s: B.at[s], lambda s: A.at[s, pl.ds(SPLIT, 256 - SPLIT)]),
        ),
        send_llm, recv_llm,
    )
    for copy in own:
        copy.wait()

    own_rows = pl.ds(pl.multiple_of(c * 48, 16), 48)
    other_rows = pl.ds(pl.multiple_of(o * 48, 16), 48)
    image_other = remote(img2.at[o], henc.at[own_rows], misc_s.at[0], misc_r.at[0], other)

    @pl.when(x == 2)
    def _():
        spread = lax.broadcasted_iota(jnp.int32, (256, 128), 0)
        lane = lax.broadcasted_iota(jnp.int32, (256, 128), 1)
        for b in range(2 * BLOCKS):
            base = 100 * b // 128 * 128
            width = min(256, 3200 - base)
            pick = (spread == lane + (100 * b - base)) & (lane < 100)
            pick = jnp.where(pick, 1.0, 0.0).astype(BF16)[0:width]
            block = matmul(image[:, base : base + width], pick).astype(BF16)
            img2[b % 2, :, b // 2 * 128 : (b // 2 + 1) * 128] = block
        image_other.start()
        henc[own_rows, :] = img2[c]

    @pl.when(x == 2)
    def _():
        for source in (0, 1):
            for copy in gathered(source):
                copy.wait_recv()
        start, steps, finish = relay(
            ((lambda s: E1.at[s],), (lambda s: E2.at[s],)), send_enc, recv_enc
        )
        start()
        for step in steps:
            step()
        finish()

    @pl.when(x == 3)
    def _():
        for copy in gathered(2):
            copy.wait_recv()
        start, steps, finish = relay(
            (
                (lambda s: E1.at[s], lambda s: C1.at[s]),
                (lambda s: E2.at[s], lambda s: C2.at[s]),
            ),
            send_enc, recv_enc,
        )
        start()
        for step in steps:
            step()
        finish()

    llm_start()

    def text_local(j):
        return pltpu.make_async_copy(
            text.at[:, pl.ds(pl.multiple_of(j * 512 + c * 256, 256), 256)],
            h0.at[c, :, pl.ds(j * 256, 256)],
            text_l.at[j],
        )

    def text_other(j):
        return remote(
            text.at[:, pl.ds(pl.multiple_of(j * 512 + o * 256, 256), 256)],
            h0.at[c, :, pl.ds(j * 256, 256)],
            text_s.at[j], text_r.at[j], other,
        )

    def text_came(j):
        return remote(
            text.at[:, pl.ds(0, 256)],
            h0.at[o, :, pl.ds(j * 256, 256)],
            text_s.at[j], text_r.at[j], other,
        )

    marks_other = remote(ohb.at[c], ohb.at[c], misc_s.at[1], misc_r.at[1], other)

    @pl.when(x == 0)
    def _():
        spot = jnp.full((1, 128), -1.0, F32)
        for m in range(3):
            j = lax.broadcasted_iota(jnp.int32, (16, 128), 0)
            at = lax.broadcasted_iota(jnp.int32, (16, 128), 1)
            pick = jnp.where(at == j + (m * 16 + c * 48), 1.0, 0.0).astype(BF16)
            rows = (positions[m : m + 1, :] + (64 * m + 1)).astype(F32).astype(BF16)
            spot += matmul(jnp.broadcast_to(rows, (16, 16)), pick)[0:1]
        row = lax.broadcasted_iota(jnp.int32, (192, 128), 0).astype(F32)
        ohb[c] = jnp.where(row == spot, 1.0, 0.0).astype(BF16)
        marks_other.start()
        for j in range(BLOCKS):
            text_local(j).start()
            text_other(j).start()

    def projected(slot, product):
        h = henc[...]
        es[slot, :, 0:128] = product(h)
        squares = jnp.zeros((96, 128), F32)
        for j in range(BLOCKS):
            part = h[:, j * 128 : (j + 1) * 128].astype(F32)
            squares += part * part
        es[slot, :, 128:256] = squares
        total = exchange(es.at[slot], er.at[slot], xe_s, xe_r, slot)
        scale = lax.rsqrt(
            jnp.sum(total[:, 128:256], axis=-1, keepdims=True) * (1.0 / 3200) + EPSILON
        )
        return gelu(total[:, 0:128] * scale).astype(BF16)

    passed = remote(henc, henc, misc_s.at[2], misc_r.at[2], x_next)
    pictures = remote(
        imgrows.at[pl.ds(0, 96)], imgrows.at[pl.ds(0, 96)], misc_s.at[3], misc_r.at[3], x_next
    )

    def encoder(plane):
        @pl.when(x == plane)
        def _():
            if plane == 2:
                image_other.wait_send()
                remote(
                    img2.at[c], henc.at[other_rows], misc_s.at[0], misc_r.at[0], other
                ).wait_recv()
            else:
                passed.wait_recv()

            def layer(l, _):
                k, half = l // 2, lax.rem(l, 2)
                weight = E1[pl.ds(half * BLOCKS, BLOCKS), k].reshape(BLOCKS * 128, 128)
                activated = projected(half, lambda h: matmul(h, weight))
                for j in range(BLOCKS):
                    branch = matmul_t(activated, E2[half * BLOCKS + j, k])
                    span = slice(j * 128, (j + 1) * 128)
                    henc[:, span] = (henc[:, span].astype(F32) + branch).astype(BF16)
                return 0

            lax.fori_loop(0, 4, layer, 0)
            if plane == 2:
                passed.start()
            else:

                def to_latent(h):
                    total = jnp.zeros((96, 128), F32)
                    for j in range(BLOCKS):
                        total += matmul_t(h[:, j * 128 : (j + 1) * 128], C1[j])
                    return total

                latent = projected(0, to_latent)[:, 0:64]
                for j in range(BLOCKS):
                    imgrows[0:96, j * 256 : (j + 1) * 256] = matmul(latent, C2[j]).astype(BF16)
                pictures.start()

    def cols(j):
        return slice(j * 256, (j + 1) * 256)

    def first_state():
        @pl.when(x == 0)
        def _():
            marks_other.wait_send()
            remote(ohb.at[o], ohb.at[o], misc_s.at[1], misc_r.at[1], other).wait_recv()
            for j in range(BLOCKS):
                text_local(j).wait()
                text_other(j).wait_send()
                text_came(j).wait_recv()
            imgrows[96:128, :] = jnp.zeros((32, BLOCKS * 256), BF16)
            pictures.wait_recv()

            def place(n, _):
                k = n + jnp.where(n < 2, 2 * z_hi, 2)
                rows = pl.ds(pl.multiple_of(32 * k, 32), 32)
                both = pl.ds(pl.multiple_of(64 * k, 64), 64)
                marks = jnp.concatenate([ohb[0, rows, :], ohb[1, rows, :]], axis=0)
                hit = jnp.sum(marks.astype(F32), axis=-1, keepdims=True) > 0.5
                for j in range(BLOCKS):
                    placed = matmul(marks, imgrows[:, cols(j)])
                    words = jnp.concatenate([h0[0, rows, cols(j)], h0[1, rows, cols(j)]], axis=0)
                    hin[both, cols(j)] = jnp.where(hit, placed, words.astype(F32)).astype(BF16)
                return 0

            lax.fori_loop(0, 4, place, 0)

    encoder(2)
    for number, step in enumerate(llm_steps):
        if number == TURN:
            encoder(3)
        if number == len(llm_steps) - 12:
            first_state()
        step()
    llm_finish()

    @pl.when(x == 3)
    def _():
        pictures.wait_send()

    @pl.when(x == 2)
    def _():
        passed.wait_send()

    for source in range(3):

        @pl.when(x == source)
        def _():
            for copy in gathered(source):
                copy.wait_send()

    def folded(v):
        return v[:, 0:128] * v[:, 0:128] + v[:, 128:256] * v[:, 128:256]

    def activation(slot, acc, squares, meanwhile):
        xs[slot, :, 0:512] = acc
        xs[slot, :, 512:640] = squares
        copy = remote(xs.at[slot], xr.at[slot], x_s.at[slot], x_r.at[slot], other)
        copy.start()
        meanwhile()
        copy.wait_recv()
        squares += xr[slot, :, 512:640]
        scale = lax.rsqrt(jnp.sum(squares, axis=-1, keepdims=True) * (1.0 / 8192) + EPSILON)
        activated = silu((acc + xr[slot, :, 0:512]) * scale).astype(BF16)
        copy.wait_send()
        return activated

    def span_of(start):
        return pl.ds(pl.multiple_of(start, 32), 32)

    def flow(k, start, part):
        span = hin.at[
            pl.ds(pl.multiple_of(2 * start, 64), 64), pl.ds(part * 1024, 1024)
        ]
        return remote(span, span, flow_s.at[k, part], flow_r.at[k, part], x_next)

    def result(k, start):
        rows = span_of(start)
        return remote(osend.at[rows], orecv.at[rows], out_s.at[k], out_r.at[k], other)

    def emit(k, start, source, base):
        mine = pl.ds(pl.multiple_of(base + c * 32, 32), 32)
        theirs = pl.ds(pl.multiple_of(base + o * 32, 32), 32)
        rows = span_of(start)
        osend[rows, :] = source[theirs, :]
        result(k, start).start()
        for j in range(BLOCKS):
            out[rows, pl.ds(pl.multiple_of(j * 512 + c * 256, 256), 256)] = source[mine, cols(j)]

    def merge(k, start):
        result(k, start).wait_recv()
        rows = span_of(start)
        for j in range(BLOCKS):
            out[rows, pl.ds(pl.multiple_of(j * 512 + o * 256, 256), 256)] = orecv[rows, cols(j)]

    def crossing(n):
        k = min(n, 1)
        span = pl.ds((0, 0, 2048)[n], (4096, 2048, 2048)[n])
        return remote(zout.at[k, :, span], zin.at[k, :, span], z_s.at[n], z_r.at[n], opposite)

    def leg(n, part):
        near = pl.ds(part * 1024, 1024)
        far = pl.ds(2048 + part * 1024, 1024)
        src = (zout.at[1, :, far], zby.at[0, :, near], zby.at[1, :, near])[n]
        dst = (zby.at[0, :, near], zby.at[1, :, near], zin.at[1, :, far])[n]
        to = (x_next, opposite, x_last)[n]
        return remote(src, dst, by_s.at[n, part], by_r.at[n, part], to)

    def cross(k):
        if k == 0:
            crossing(0).start()
            return
        crossing(1).start()

        @pl.when(x < 3)
        def _():
            crossing(2).start()

        @pl.when(x == 3)
        def _():
            for part in range(2):
                leg(0, part).start()

    def chunk(k, start, halved, sent_last):
        base = pl.multiple_of(2 * start, 64)
        rows = span_of(start)
        both = pl.ds(base, 64)

        def give(layer):
            @pl.when(z_hi == layer)
            def _():
                emit(k, start, hin, base)

            if halved:

                @pl.when(z_hi != layer)
                def _():
                    zout[k] = hin[both, :]
                    cross(k)

        acc, squares = jnp.zeros((64, 512), F32), jnp.zeros((64, 128), F32)
        for part in range(4):

            @pl.when(x > 0)
            def _():
                flow(k, start, part).wait_recv()

            for j in range(4 * part, 4 * part + 4):
                h = hin[both, cols(j)]
                acc, squares = acc + matmul(h, A[j]), squares + folded(h.astype(F32))
        a = activation(0, acc, squares, lambda: None)
        acc, squares = jnp.zeros((64, 512), F32), jnp.zeros((64, 128), F32)
        for j in range(BLOCKS):
            h = (hin[both, cols(j)].astype(F32) + matmul(a, B[j])).astype(BF16)
            hin[both, cols(j)] = h
            acc, squares = acc + matmul(h, A[BLOCKS + j]), squares + folded(h.astype(F32))
        b = activation(1, acc, squares, lambda: give(0))
        for part in range(4):
            for j in range(4 * part, 4 * part + 4):
                h = hin[both, cols(j)].astype(F32) + matmul(b, B[BLOCKS + j])
                hin[both, cols(j)] = h.astype(BF16)

            @pl.when(x < 3)
            def _():
                sent_last(part)
                flow(k, start, part).start()

        give(1)

    first = z_hi * 64
    across_first = 64 - first
    chunk(0, first, True, lambda part: None)
    chunk(1, first + 32, True, lambda part: flow(0, first, part).wait_send())
    merge(0, first)

    def shared(k, _):
        def sent_last(part):
            @pl.when(k == 2)
            def _():
                flow(1, first + 32, part).wait_send()

            @pl.when(k > 2)
            def _():
                flow(k - 1, 32 * k + 32, part).wait_send()

        chunk(k, 32 * k + 64, False, sent_last)

        @pl.when(k == 2)
        def _():
            merge(1, first + 32)

        @pl.when(k > 2)
        def _():
            merge(k - 1, 32 * k + 32)

        return 0

    lax.fori_loop(2, 4, shared, 0)
    crossing(0).wait_recv()
    emit(4, across_first, zin.at[0], 0)
    merge(3, 160)
    crossing(1).wait_recv()

    @pl.when(x < 3)
    def _():
        crossing(2).wait_recv()

    @pl.when(x == 3)
    def _():
        for part in range(2):
            leg(2, part).wait_recv()

    emit(5, across_first + 32, zin.at[1], 0)
    for k in range(2):
        merge(4 + k, across_first + 32 * k)
        result(k, first + 32 * k).wait_send()
        result(2 + k, 128 + 32 * k).wait_send()
        result(4 + k, across_first + 32 * k).wait_send()
        crossing(k).wait_send()

    @pl.when(x < 3)
    def _():
        crossing(2).wait_send()

    @pl.when(x == 3)
    def _():
        for part in range(2):
            leg(0, part).wait_send()

    @pl.when(x == 0)
    def _():
        for n in (0, 1):
            for part in range(2):
                leg(n, part).wait_recv()
                leg(n + 1, part).start()
        for n in (1, 2):
            for part in range(2):
                leg(n, part).wait_send()

    @pl.when(x < 3)
    def _():
        for part in range(4):
            flow(3, 160, part).wait_send()


def local(text, image, positions, enc_in, enc_out, conn_in, conn_out, llm_in, llm_out):
    hbm_spec = pl.BlockSpec(memory_space=pltpu.HBM)
    vmem_spec = pl.BlockSpec(memory_space=pltpu.VMEM)
    dma = pltpu.SemaphoreType.DMA
    hidden = pl.pallas_call(
        kernel,
        out_shape=jax.ShapeDtypeStruct((192, 8192), BF16),
        in_specs=[hbm_spec] + [vmem_spec] * 6 + [hbm_spec] * 2,
        out_specs=vmem_spec,
        scratch_shapes=[
            pltpu.VMEM((32, 256, 512), BF16),
            pltpu.VMEM((32, 512, 256), BF16),
            pltpu.VMEM((32, 2, 128, 128), BF16),
            pltpu.VMEM((32, 2, 128, 128), BF16),
            pltpu.VMEM((32, 128, 128), BF16),
            pltpu.VMEM((32, 64, 256), BF16),
            pltpu.VMEM((2, 128, 128), BF16),
            pltpu.VMEM((2, 192, 4096), BF16),
            pltpu.VMEM((2, 192, 128), BF16),
            pltpu.VMEM((2, 48, 2048), BF16),
            pltpu.VMEM((96, 2048), BF16),
            pltpu.VMEM((128, 4096), BF16),
            pltpu.VMEM((2, 64, 640), F32),
            pltpu.VMEM((2, 64, 640), F32),
            pltpu.VMEM((2, 96, 256), F32),
            pltpu.VMEM((2, 96, 256), F32),
            pltpu.VMEM((384, 4096), BF16),
            pltpu.VMEM((192, 4096), BF16),
            pltpu.VMEM((192, 4096), BF16),
            pltpu.VMEM((2, 64, 4096), BF16),
            pltpu.VMEM((2, 64, 4096), BF16),
            pltpu.VMEM((2, 64, 2048), BF16),
            dma((3, 31)),
            dma((3, 32)),
            dma((4, 31)),
            dma((4, 32)),
            dma((2,)),
            dma((2, 2)),
            dma((2,)),
            dma((16,)),
            dma((16,)),
            dma((16,)),
            dma((4,)),
            dma((4,)),
            dma((2,)),
            dma((2,)),
            dma((2,)),
            dma((2,)),
            dma((4, 4)),
            dma((4, 4)),
            dma((6,)),
            dma((6,)),
            dma((3,)),
            dma((3,)),
            dma((3, 2)),
            dma((3, 2)),
        ],
        compiler_params=pltpu.CompilerParams(
            collective_id=0, has_side_effects=True, vmem_limit_bytes=50 * 1024 * 1024
        ),
        cost_estimate=pl.CostEstimate(
            flops=14_000_000_000, bytes_accessed=16_000_000, transcendentals=1_000_000
        ),
    )(
        text, image, positions, enc_in[0], enc_out[0].T, conn_in.T, conn_out, llm_in[0], llm_out[0]
    )
    return hidden[None]


def solution(mesh):
    return jax.shard_map(
        local,
        mesh=mesh,
        in_specs=(
            P("dp", None),
            P("dp", None),
            P("dp", None),
            P("section", "dp", None),
            P("section", None, "dp"),
            P("dp", None),
            P(None, "dp"),
            P("section", "dp", None),
            P("section", None, "dp"),
        ),
        out_specs=P("section", "dp", None),
        check_vma=False,
    )
```
